256 devices in a mesh: dp: 16 (over z_lo, x, core), node: 16 (over z_hi, y).
Axes of the slice: x: 4, y: 4, z: 8 (z_hi: 4, z_lo: 2; z = z_hi * 2 + z_lo), core: 2. Of those that a mesh axis runs over, the one named last changes fastest.
Arguments:
- tokens: bfloat16 [131072, 3584], P(('dp', 'node')), may hold values from -6 to 6
- slot_tokens: int32 [65536], P(('dp', 'node')), may hold values from 0 to 511, as said below
- slot_counts: int32 [256], P(('dp', 'node')), may hold values from 64 to 256, as said below
- route_weight: float32 [65536], P(('dp', 'node')), may hold values from 0.25 to 1.5
- cotangent: bfloat16 [65536, 1024], P(('dp', 'node')), may hold values from -6 to 6
- weights: bfloat16 [2, 1024, 3584], P(None, 'node'), may hold values from -0.09375 to 0.09375
Outputs:
- activation: bfloat16 [65536, 1024], P(('dp', 'node'))
- token_grad: bfloat16 [131072, 3584], P(('dp', 'node'))
- weight_grad: float32 [2, 1024, 3584], P(None, 'node')
The draws below stay inside these ranges and needn't reach their ends.
Inputs may be any that keep to these rules, and one draw needn't show every extreme that they name: `slot_tokens`: within each device's block of 256 slots the entries are distinct token indices of that device. `slot_counts`: some device uses all 256 of its slots in every draw.
All inputs are finite; a program needn't handle non-finite values.
Results may differ from the reference program's by a relative error of at most 0.015.
Values may be sent and summed in bfloat16 or wider, within the bound.
No kernel may reach another device: no remote copies, remote signals or barrier semaphores. Data moves between devices by JAX's collectives and lax.ppermute only.
A program may use at most 128 MiB of HBM per device.

```python
import jax
import jax.numpy as jnp
from jax import lax

D = 3584
H = 1024
TOK_DEV = 512
CAP = 256
TOKENS = 131072
SLOTS = 65536


def draw_slot_tokens(key, part):
    key = jax.random.fold_in(key, 11)
    count = TOKENS // TOK_DEV
    keys = jax.random.split(key, count)
    orders = jax.vmap(lambda single: jax.random.permutation(single, TOK_DEV))(keys)
    return orders[:, :CAP].reshape(-1).astype(jnp.int32)


def draw_slot_counts(key, part):
    key = jax.random.fold_in(key, 23)
    count = TOKENS // TOK_DEV
    values = jax.random.randint(key, (count,), CAP // 4, CAP + 1)
    fullest = jax.random.randint(jax.random.fold_in(key, 5), (), 0, count)
    return jnp.where(jnp.arange(count) == fullest, CAP, values).astype(jnp.int32)


def levels(rng, shape, pieces, least, largest):
    gain = 1.0
    for position, parts in pieces:
        draws = jax.random.uniform(jax.random.fold_in(jax.random.fold_in(rng, 6), position), (parts,), jnp.float32, least / len(pieces), largest / len(pieces))
        gain = gain * jnp.repeat(jnp.exp(draws), shape[position] // parts).reshape((-1,) + (1,) * (len(shape) - 1 - position))
    return gain


def normal_values(key, dims, spread, bound, cuts=(), held_as=jnp.bfloat16):
    level = levels(key, dims, cuts, -0.22, 0.18) if cuts else 1.0
    entries = jax.random.normal(key, dims, jnp.float32) * spread * level
    return jnp.minimum(jnp.maximum(entries, -bound), bound).astype(held_as)


def setup_inputs(seed: int = 0) -> dict:
    streams_of = jax.random.split(jax.random.key(seed), 7)
    tokens = normal_values(streams_of[0], (TOKENS, D), 1.0, 6.0, ((0, 256),))
    slot_tokens = draw_slot_tokens(jax.random.fold_in(streams_of[6], 71), 0)
    slot_counts = draw_slot_counts(jax.random.fold_in(streams_of[6], 71), 0)
    route_weight = jnp.clip(0.25 + 1.25 * jax.random.uniform(streams_of[3], (SLOTS,), jnp.float32) ** levels(streams_of[3], (SLOTS,), ((0, 256),), -0.2, 0.2), 0.25, 1.5)
    cotangent = normal_values(streams_of[4], (SLOTS, H), 1.0, 6.0, ((0, 256),))
    weights = normal_values(streams_of[5], (2, H, D), D ** -0.5, 0.09375, ((1, 16),))
    return {"tokens": tokens, "slot_tokens": slot_tokens, "slot_counts": slot_counts, "route_weight": route_weight, "cotangent": cotangent, "weights": weights}


def one_device(carry, index, tokens, slot_tokens, slot_counts, route_weight, cotangent, weights):
    slot_rows = lax.dynamic_slice_in_dim(slot_tokens, index * CAP, CAP)
    own_tokens = lax.dynamic_slice_in_dim(tokens, index * TOK_DEV, TOK_DEV, 0)
    picked = own_tokens[slot_rows]
    weight_wide = weights.astype(jnp.float32)
    pre = jnp.einsum('kd,chd->ckh', picked.astype(jnp.float32), weight_wide)
    gate = pre[0]
    upval = pre[1]
    used = (jnp.arange(CAP, dtype=jnp.int32) < slot_counts[index]).astype(jnp.float32)[:, None]
    scale = lax.dynamic_slice_in_dim(route_weight, index * CAP, CAP)[:, None]
    sigma = jax.nn.sigmoid(gate)
    activation = (used * scale * gate * sigma * upval).astype(jnp.bfloat16)
    cot_rows = lax.dynamic_slice_in_dim(cotangent, index * CAP, CAP, 0).astype(jnp.float32)
    scaled = cot_rows * scale * used
    up_grad = (scaled * gate * sigma).astype(jnp.bfloat16)
    gate_grad = (scaled * upval * sigma * (1.0 + gate * (1.0 - sigma))).astype(jnp.bfloat16)
    stacked = jnp.stack([gate_grad, up_grad]).astype(jnp.float32)
    slot_grad = jnp.einsum('ckh,chd->kd', stacked, weight_wide)
    token_grad = jnp.zeros((TOK_DEV, D), jnp.float32).at[slot_rows].add(slot_grad).astype(jnp.bfloat16)
    factor = 1.0 / (SLOTS ** 0.5)
    partial_term = (jnp.einsum('kd,ckh->chd', picked.astype(jnp.float32), stacked) * factor).astype(jnp.bfloat16)
    partial_term = lax.optimization_barrier(partial_term)
    return carry + partial_term.astype(jnp.float32), (activation, token_grad)


def reference(tokens, slot_tokens, slot_counts, route_weight, cotangent, weights):
    count = TOKENS // TOK_DEV
    start = jnp.zeros((2, H, D), jnp.float32)
    step = lambda carry, index: one_device(carry, index, tokens, slot_tokens, slot_counts, route_weight, cotangent, weights)
    weight_grad, outputs = lax.scan(step, start, jnp.arange(count, dtype=jnp.int32))
    activation = outputs[0].reshape(count * CAP, H)
    token_grad = outputs[1].reshape(count * TOK_DEV, D)
    return activation, token_grad, weight_grad
```

```python
import jax
import jax.numpy as jnp
import numpy as np
from jax import lax
from jax.sharding import Mesh
from jax.sharding import PartitionSpec as P

AXES = ("zl", "x", "c", "zh", "y")
SIZES = (2, 4, 2, 4, 4)
MASKS = ((1, 3), (3, 1))
BF = jnp.bfloat16
F32 = jnp.float32


def pairs(axis, stage):
    index = np.arange(256).reshape(SIZES)
    out = []
    for source in range(256):
        place = list(np.unravel_index(source, SIZES))
        at = AXES.index(axis)
        place[at] ^= MASKS[place[2]][stage] if SIZES[at] == 4 else 1
        out.append((source, int(index[tuple(place)])))
    return out


def swap(value, axis, stage=0):
    return lax.ppermute(value, AXES, pairs(axis, stage))


def mask_of(core, stage):
    return jnp.where(core == 0, MASKS[0][stage], MASKS[1][stage])


STAGES_A = (("zh", 0), ("zh", 1), ("y", 0), ("y", 1), ("x", 0), ("x", 1))
STAGES_B = (("zh", 0), ("zh", 1), ("y", 0), ("y", 1))


def gather(block, stages):
    for axis, stage in stages[:-1]:
        block = jnp.concatenate([block, swap(block, axis, stage)], axis=0)
    return block, swap(block, *stages[-1])


def add(a, b):
    return (a.astype(F32) + b.astype(F32)).astype(BF)


def scatter_sum(own, other, stages):
    total = add(own, swap(other, *stages[-1]))
    for axis, stage in stages[-2::-1]:
        half = total.shape[0] // 2
        total = add(total[:half], swap(total[half:], axis, stage))
    return total


def hidden_of_lanes(core, x, zh, y):
    row = jnp.arange(512, dtype=jnp.int32)

    def source(place, low, high):
        place = place ^ jnp.where(row & low != 0, mask_of(core, 0), 0)
        return place ^ jnp.where(row & high != 0, mask_of(core, 1), 0)

    a = (source(zh, 8, 16) * 4 + source(y, 32, 64)) * 64 + source(x, 128, 256) * 4
    b = (source(zh, 32, 64) * 4 + source(y, 128, 256)) * 64 + source(x, 8, 16) * 4 + 16
    return jnp.concatenate([a, b]) + core * 32 + (row[None] & 3).repeat(2, 0).reshape(-1)


def local(tokens, slot_tokens, slot_counts, route_weight, cotangent, weights):
    core, x = lax.axis_index("c"), lax.axis_index("x")
    zh, y = lax.axis_index("zh"), lax.axis_index("y")
    slots = slot_tokens.shape[0]
    width = tokens.shape[1]
    factor = 1.0 / (slots * 256) ** 0.5

    half = lax.dynamic_slice_in_dim(weights, core * 32, 32, 1)
    groups = half.reshape(2, 8, 4, width).transpose(1, 0, 2, 3).reshape(8, 8, width)
    order = [x, x ^ mask_of(core, 0), x ^ mask_of(core, 1), x ^ 2]
    a_own = lax.dynamic_index_in_dim(groups, x, 0, False)
    b_own = jnp.concatenate([lax.dynamic_index_in_dim(groups, 4 + g, 0, False) for g in order])
    a_pieces = gather(a_own, STAGES_A)
    b_pieces = gather(b_own, STAGES_B)

    pick = (slot_tokens[:, None] == jnp.arange(tokens.shape[0], dtype=jnp.int32)[None]).astype(BF)
    picked_own = jnp.dot(pick, tokens, preferred_element_type=F32).astype(BF)
    used = (jnp.arange(slots, dtype=jnp.int32) < slot_counts[0]).astype(F32)
    scale_own = (route_weight * used).reshape(2, 128)
    picked_other = swap(picked_own, "c")
    cot_other = swap(cotangent, "c")
    scale_other = swap(scale_own, "c")
    picked = jnp.concatenate([picked_own, picked_other], axis=0)
    scale = jnp.concatenate([scale_own, scale_other], axis=0).reshape(2 * slots, 1)

    lanes = lax.optimization_barrier(hidden_of_lanes(core, x, zh, y))
    lanes_other = lax.optimization_barrier(hidden_of_lanes(1 - core, x, zh, y))
    hidden = jnp.arange(1024, dtype=jnp.int32)
    spread = (hidden[:, None] == lanes[None]).astype(BF)
    cot = jnp.dot(
        jnp.concatenate([cotangent, cot_other], axis=0), spread, preferred_element_type=F32
    )

    is_gate = (jnp.arange(256, dtype=jnp.int32) & 4 == 0)[None]

    def work(piece, cot):
        pre = jnp.einsum("kd,hd->kh", picked, piece, preferred_element_type=F32)
        gate, upval = pre, jnp.roll(pre, -4, axis=1)
        sigma = jax.nn.sigmoid(gate)
        activation = jnp.where(is_gate, scale * gate * sigma * upval, 0.0).astype(BF)
        scaled = cot * scale
        up_grad = scaled * gate * sigma
        gate_grad = scaled * upval * sigma * (1.0 + gate * (1.0 - sigma))
        grads = jnp.where(is_gate, gate_grad, jnp.roll(up_grad, 4, axis=1)).astype(BF)
        return activation, grads

    def weight_part(grads):
        part = jnp.einsum("kh,kd->hd", grads, picked, preferred_element_type=F32)
        return (part * factor).astype(BF)

    done = [
        work(piece, cot[:, 256 * n : 256 * (n + 1)])
        for n, piece in enumerate((*a_pieces, *b_pieces))
    ]
    grads = [g for _, g in done]
    b_sum = scatter_sum(weight_part(grads[2]), weight_part(grads[3]), STAGES_B)
    a_sum = scatter_sum(weight_part(grads[0]), weight_part(grads[1]), STAGES_A)
    b_sum = add(b_sum[:16], swap(b_sum[16:], "x", 1))
    b_sum = add(b_sum[:8], swap(b_sum[8:], "x", 0))

    act = jnp.concatenate([a for a, _ in done], axis=1)
    act_other = swap(act[slots:], "c")
    gate_lane = (jnp.arange(1024, dtype=jnp.int32) & 4 == 0)[:, None]
    back = ((hidden[None] == lanes[:, None]) & gate_lane).astype(BF)
    back_other = ((hidden[None] == lanes_other[:, None]) & gate_lane).astype(BF)
    activation = (
        jnp.dot(act[:slots], back, preferred_element_type=F32)
        + jnp.dot(act_other, back_other, preferred_element_type=F32)
    ).astype(BF)

    slot_grad = jnp.dot(
        jnp.concatenate(grads, axis=1),
        jnp.concatenate([*a_pieces, *b_pieces], axis=0),
        preferred_element_type=F32,
    )
    grad_other = swap(slot_grad[slots:].astype(BF), "c")
    slot_grad = (slot_grad[:slots] + grad_other.astype(F32)).astype(BF)
    token_grad = jnp.dot(pick.T, slot_grad, preferred_element_type=F32).astype(BF)

    total = jnp.concatenate([a_sum, b_sum], axis=0)
    total = total.astype(F32) + swap(total, "zl").astype(F32)
    total = total.astype(BF).reshape(1, 2, 8, width)
    for stage in range(2):
        total = jnp.concatenate([total, swap(total, "x", stage)], axis=0)
    where = [sum(i * (g == n) for i, g in enumerate(order)) for n in range(4)]
    total = jnp.stack([lax.dynamic_index_in_dim(total, i, 0, False) for i in where])
    total = total.transpose(1, 0, 2, 3).reshape(8, 2, 4, width)
    total = total.transpose(1, 0, 2, 3).reshape(2, 32, width)
    other = swap(total, "c")
    first = jnp.where(core == 0, total, other)
    second = jnp.where(core == 0, other, total)
    weight_grad = jnp.concatenate([first, second], axis=1).astype(F32)
    return activation, token_grad, weight_grad


def solution(mesh):
    fine = Mesh(mesh.devices.reshape(SIZES), AXES)
    rows = P(AXES, None)
    panel = P(None, ("zh", "y"), None)
    return jax.shard_map(
        local,
        mesh=fine,
        in_specs=(rows, P(AXES), P(AXES), P(AXES), rows, panel),
        out_specs=(rows, rows, panel),
        check_vma=False,
    )
```

```python
import functools

import jax
import jax.numpy as jnp
import numpy as np
from jax import lax
from jax.experimental import pallas as pl
from jax.experimental.pallas import tpu as pltpu
from jax.sharding import Mesh
from jax.sharding import PartitionSpec as P

AXES = ("zl", "x", "c", "zh", "y")
SIZES = (2, 4, 2, 4, 4)
MASKS = ((1, 3), (3, 1))
BF = jnp.bfloat16
F32 = jnp.float32
VMEM = pl.BlockSpec(memory_space=pltpu.VMEM)
ANY = pl.BlockSpec(memory_space=pl.ANY)


def pairs(axis, stage):
    index = np.arange(256).reshape(SIZES)
    out = []
    for source in range(256):
        place = list(np.unravel_index(source, SIZES))
        at = AXES.index(axis)
        place[at] ^= MASKS[place[2]][stage] if SIZES[at] == 4 else 1
        out.append((source, int(index[tuple(place)])))
    return out


def swap(value, axis, stage=0):
    return lax.ppermute(value, AXES, pairs(axis, stage))


def mask_of(core, stage):
    return jnp.where(core == 0, MASKS[0][stage], MASKS[1][stage])


def turned(core, place, index):
    place = place ^ jnp.where(index & 1 != 0, mask_of(core, 0), 0)
    return place ^ jnp.where(index & 2 != 0, mask_of(core, 1), 0)


def call(kernel, out, *args, after=(), flops=0):
    size = sum(a.size * a.dtype.itemsize for a in (*args, *out))

    def body(*refs):
        refs = refs[: len(args)] + refs[len(args) + len(after) :]
        kernel(*refs)

    return pl.pallas_call(
        body,
        out_shape=out,
        in_specs=[VMEM] * len(args) + [ANY] * len(after),
        out_specs=[VMEM] * len(out),
        compiler_params=pltpu.CompilerParams(vmem_limit_bytes=40 * 2**20),
        cost_estimate=pl.CostEstimate(flops=flops, bytes_accessed=size, transcendentals=0),
    )(*args, *after)


def like(rows, width, dtype=BF):
    return jax.ShapeDtypeStruct((rows, width), dtype)


def join(*blocks, after=()):
    def kernel(*refs):
        for n in range(len(blocks) // 2):
            one, two = refs[2 * n], refs[2 * n + 1]
            out = refs[len(blocks) + n]
            if one.shape[0] % 16:
                both = jnp.concatenate([one[...].astype(F32), two[...].astype(F32)], axis=0)
                out[...] = both.astype(BF)
            else:
                out[: one.shape[0]] = one[...]
                out[one.shape[0] :] = two[...]

    out = [like(2 * b.shape[0], b.shape[1]) for b in blocks[::2]]
    return call(kernel, out, *blocks, after=after)


def add(*blocks, split=True, after=()):
    def kernel(*refs):
        outs = refs[len(blocks) :]
        for n in range(len(blocks) // 2):
            total = refs[2 * n][...].astype(F32) + refs[2 * n + 1][...].astype(F32)
            if split:
                half = total.shape[0] // 2
                outs[2 * n][...] = total[:half].astype(BF)
                outs[2 * n + 1][...] = total[half:].astype(BF)
            else:
                outs[n][...] = total.astype(BF)

    out = []
    for b in blocks[::2]:
        out += [like(b.shape[0] // 2, b.shape[1])] * 2 if split else [like(*b.shape)]
    return call(kernel, out, *blocks, after=after)


def hidden_of_lanes(core, x, zh, y):
    row = jnp.arange(512, dtype=jnp.int32)
    at = functools.partial(turned, core)
    a = (at(zh, row >> 3) * 4 + at(y, row >> 5)) * 64 + at(x, row >> 7) * 4
    b = (at(zh, row >> 5) * 4 + at(y, row >> 7)) * 64 + at(x, row >> 3) * 4 + 16
    return jnp.concatenate([a, b]) + core * 32 + jnp.concatenate([row, row]) % 4


def hidden_work(pieces, picked, cots, scale, after=()):
    rows = picked.shape[0]

    def kernel(*refs):
        picked_ref, scale_ref = refs[:2]
        inner = refs[2:]
        for n in range(len(pieces)):
            piece, cot = inner[2 * n], inner[2 * n + 1]
            act, grad = inner[2 * len(pieces) + 2 * n :][:2]
            is_gate = lax.broadcasted_iota(jnp.int32, (1, 256), 1) & 4 == 0
            for r in range(0, rows, 128):
                here = pl.ds(r, 128)
                pre = lax.dot_general(
                    picked_ref[here, :],
                    piece[...],
                    (((1,), (1,)), ((), ())),
                    preferred_element_type=F32,
                )
                gate, upval = pre, pltpu.roll(pre, 252, 1)
                weight = scale_ref[here, :]
                sigma = jax.nn.sigmoid(gate)
                act[here, :] = jnp.where(is_gate, weight * gate * sigma * upval, 0.0).astype(BF)
                scaled = cot[here, :].astype(F32) * weight
                up_grad = scaled * gate * sigma
                gate_grad = scaled * upval * sigma * (1.0 + gate * (1.0 - sigma))
                both = jnp.where(is_gate, gate_grad, pltpu.roll(up_grad, 4, 1))
                grad[here, :] = both.astype(BF)

    args = [v for pair in zip(pieces, cots) for v in pair]
    out = [like(rows, 256)] * (2 * len(pieces))
    flops = 2 * rows * 256 * picked.shape[1] * len(pieces)
    out = call(kernel, out, picked, scale, *args, after=after, flops=flops)
    return out[::2], out[1::2]


def weight_part(grads, picked, factor, after=()):
    width = picked.shape[1]

    def kernel(picked_ref, *refs):
        for n in range(len(grads)):
            for column in range(0, width, 512):
                here = pl.ds(column, 512)
                part = lax.dot_general(
                    refs[n][...],
                    picked_ref[:, here],
                    (((0,), (0,)), ((), ())),
                    preferred_element_type=F32,
                )
                refs[len(grads) + n][:, here] = (part * factor).astype(BF)

    flops = 2 * picked.size * 256 * len(grads)
    return call(
        kernel, [like(256, width)] * len(grads), picked, *grads, after=after, flops=flops
    )


def local(tokens, slot_tokens, slot_counts, route_weight, cotangent, weights):
    core, x = lax.axis_index("c"), lax.axis_index("x")
    zh, y = lax.axis_index("zh"), lax.axis_index("y")
    slots = slot_tokens.shape[0]
    width = tokens.shape[1]
    factor = 1.0 / (slots * 256) ** 0.5

    row = jnp.arange(40, dtype=jnp.int32)
    group = jnp.where(row < 8, x, 4 + turned(core, x, (row >> 3) - 1))
    wanted = ((row >> 2) & 1) * 64 + core * 32 + group * 4 + row % 4
    choose = (wanted[:, None] == jnp.arange(128, dtype=jnp.int32)[None]).astype(BF)
    own = jnp.dot(choose, weights.reshape(128, width), preferred_element_type=F32).astype(BF)
    a, b = own[:8], own[8:]

    pick = (slot_tokens[:, None] == jnp.arange(tokens.shape[0], dtype=jnp.int32)[None]).astype(BF)
    picked_own = jnp.dot(pick, tokens, preferred_element_type=F32).astype(BF)
    used = (jnp.arange(slots, dtype=jnp.int32) < slot_counts[0]).astype(F32)
    scale_own = (route_weight * used).reshape(2, 128)

    (a,) = join(a, swap(a, "zh", 0))
    (a,) = join(a, swap(a, "zh", 1))
    picked_other = swap(picked_own, "c")
    a, b = join(a, swap(a, "y", 0), b, swap(b, "zh", 0), after=[picked_other])
    cot_other = swap(cotangent, "c")
    scale_other = swap(scale_own, "c")
    a, b = join(a, swap(a, "y", 1), b, swap(b, "zh", 1), after=[cot_other, scale_other])
    a, b = join(a, swap(a, "x", 0), b, swap(b, "y", 0))
    a_new, b_new = swap(a, "x", 1), swap(b, "y", 1)

    picked = jnp.concatenate([picked_own, picked_other], axis=0)
    scale = jnp.concatenate([scale_own, scale_other], axis=0).reshape(2 * slots, 1)
    lanes = lax.optimization_barrier(hidden_of_lanes(core, x, zh, y))
    lanes_other = lax.optimization_barrier(hidden_of_lanes(1 - core, x, zh, y))
    hidden = jnp.arange(1024, dtype=jnp.int32)
    spread = (hidden[:, None] == lanes[None]).astype(BF)
    cot = jnp.dot(
        jnp.concatenate([cotangent, cot_other], axis=0), spread, preferred_element_type=F32
    ).astype(BF)
    cots = [cot[:, 256 * n : 256 * (n + 1)] for n in range(4)]

    acts_old, grads_old = hidden_work([a, b], picked, cots[::2], scale)
    acts_new, grads_new = hidden_work([a_new, b_new], picked, cots[1::2], scale)

    a_send, b_send = weight_part(grads_new, picked, factor)
    a_own, b_own = weight_part(grads_old, picked, factor)
    a_own, a_send, b_own, b_send = add(a_own, swap(a_send, "x", 1), b_own, swap(b_send, "y", 1))
    for one, two in (
        (("x", 0), ("y", 0)),
        (("y", 1), ("zh", 1)),
        (("y", 0), ("zh", 0)),
        (("zh", 1), ("x", 1)),
    ):
        a_own, a_send, b_own, b_send = add(a_own, swap(a_send, *one), b_own, swap(b_send, *two))
    a_own, b_own = add(a_own, swap(a_send, "zh", 0), b_own, swap(b_send, "x", 0), split=False)
    (total,) = join(a_own, b_own)
    (total,) = add(total, swap(total, "zl"), split=False)
    (total,) = join(total, swap(total, "x", 0))
    (total,) = join(total, swap(total, "x", 1))
    other = swap(total, "c")
    column = jnp.arange(128, dtype=jnp.int32)
    holder = jnp.where(column < 64, core, 1 - core)
    group = ((column >> 3) & 1) * 4 + turned(holder, x, column >> 4)
    place = ((column >> 2) & 1) * 64 + holder * 32 + group * 4 + column % 4
    choose = (jnp.arange(128, dtype=jnp.int32)[:, None] == place[None]).astype(BF)
    weight_grad = jnp.dot(
        choose, jnp.concatenate([total, other], axis=0), preferred_element_type=F32
    ).reshape(2, 64, width)

    act = jnp.concatenate([acts_old[0], acts_new[0], acts_old[1], acts_new[1]], axis=1)
    act_other = swap(act[slots:], "c")
    gate_lane = (jnp.arange(1024, dtype=jnp.int32) & 4 == 0)[:, None]
    back = ((hidden[None] == lanes[:, None]) & gate_lane).astype(BF)
    back_other = ((hidden[None] == lanes_other[:, None]) & gate_lane).astype(BF)
    activation = (
        jnp.dot(act[:slots], back, preferred_element_type=F32)
        + jnp.dot(act_other, back_other, preferred_element_type=F32)
    ).astype(BF)

    slot_grad = jnp.dot(
        jnp.concatenate([grads_old[0], grads_new[0], grads_old[1], grads_new[1]], axis=1),
        jnp.concatenate([a, a_new, b, b_new], axis=0),
        preferred_element_type=F32,
    )
    grad_other = swap(slot_grad[slots:].astype(BF), "c")
    slot_grad = (slot_grad[:slots] + grad_other.astype(F32)).astype(BF)
    token_grad = jnp.dot(pick.T, slot_grad, preferred_element_type=F32).astype(BF)
    return activation, token_grad, weight_grad


def solution(mesh):
    fine = Mesh(mesh.devices.reshape(SIZES), AXES)
    rows = P(AXES, None)
    panel = P(None, ("zh", "y"), None)
    return jax.shard_map(
        local,
        mesh=fine,
        in_specs=(rows, P(AXES), P(AXES), P(AXES), rows, panel),
        out_specs=(rows, rows, panel),
        check_vma=False,
    )
```

```python
import functools

import jax
import jax.numpy as jnp
import numpy as np
from jax import lax
from jax.experimental import pallas as pl
from jax.experimental.pallas import tpu as pltpu
from jax.sharding import Mesh
from jax.sharding import PartitionSpec as P

AXES = ("zl", "x", "c", "zh", "y")
SIZES = (2, 4, 2, 4, 4)
MASKS = ((1, 3), (3, 1))
BF = jnp.bfloat16
F32 = jnp.float32
VMEM = pl.BlockSpec(memory_space=pltpu.VMEM)
ANY = pl.BlockSpec(memory_space=pl.ANY)


def pairs(axis, stage):
    index = np.arange(256).reshape(SIZES)
    out = []
    for source in range(256):
        place = list(np.unravel_index(source, SIZES))
        at = AXES.index(axis)
        place[at] ^= MASKS[place[2]][stage] if SIZES[at] == 4 else 1
        out.append((source, int(index[tuple(place)])))
    return out


def swap(value, axis, stage=0):
    return lax.ppermute(value, AXES, pairs(axis, stage))


def mask_of(core, stage):
    return jnp.where(core == 0, MASKS[0][stage], MASKS[1][stage])


def turned(core, place, index):
    place = place ^ jnp.where(index & 1 != 0, mask_of(core, 0), 0)
    return place ^ jnp.where(index & 2 != 0, mask_of(core, 1), 0)


def call(kernel, out, *args, after=(), flops=0, scratch=()):
    size = sum(a.size * a.dtype.itemsize for a in (*args, *out))

    def body(*refs):
        refs = refs[: len(args)] + refs[len(args) + len(after) :]
        kernel(*refs)

    return pl.pallas_call(
        body,
        out_shape=out,
        in_specs=[VMEM] * len(args) + [ANY] * len(after),
        out_specs=[VMEM] * len(out),
        scratch_shapes=scratch,
        compiler_params=pltpu.CompilerParams(vmem_limit_bytes=40 * 2**20),
        cost_estimate=pl.CostEstimate(flops=flops, bytes_accessed=size, transcendentals=0),
    )(*args, *after)


def like(rows, width, dtype=BF):
    return jax.ShapeDtypeStruct((rows, width), dtype)


def join(*blocks, after=()):
    def kernel(*refs):
        for n in range(len(blocks) // 2):
            one, two = refs[2 * n], refs[2 * n + 1]
            out = refs[len(blocks) + n]
            if one.shape[0] % 16:
                both = jnp.concatenate([one[...].astype(F32), two[...].astype(F32)], axis=0)
                out[...] = both.astype(BF)
            else:
                out[: one.shape[0]] = one[...]
                out[one.shape[0] :] = two[...]

    out = [like(2 * b.shape[0], b.shape[1]) for b in blocks[::2]]
    return call(kernel, out, *blocks, after=after)


def halves_by_part(both):
    blocks = [both[n : n + 8] for n in range(0, both.shape[0], 8)]
    return jnp.concatenate(blocks[::2], axis=0), jnp.concatenate(blocks[1::2], axis=0)


def join_parts(one, two, after=()):
    def kernel(one_ref, two_ref, a_ref, b_ref):
        both = jnp.concatenate([one_ref[...].astype(F32), two_ref[...].astype(F32)], axis=0)
        a, b = halves_by_part(both)
        a_ref[...] = a.astype(BF)
        b_ref[...] = b.astype(BF)

    return call(kernel, [like(*one.shape)] * 2, one, two, after=after)


def add_parts(a, a_in, b, b_in, after=()):
    def kernel(a_ref, a_in_ref, b_ref, b_in_ref, own_ref, send_ref):
        sum_a = a_ref[...].astype(F32) + a_in_ref[...].astype(F32)
        sum_b = b_ref[...].astype(F32) + b_in_ref[...].astype(F32)
        blocks = []
        for n in range(0, sum_a.shape[0], 8):
            blocks += [sum_a[n : n + 8], sum_b[n : n + 8]]
        half = len(blocks) // 2
        own_ref[...] = jnp.concatenate(blocks[:half], axis=0).astype(BF)
        send_ref[...] = jnp.concatenate(blocks[half:], axis=0).astype(BF)

    return call(kernel, [like(*a.shape)] * 2, a, a_in, b, b_in, after=after)


def add(*blocks, split=True, after=()):
    def kernel(*refs):
        outs = refs[len(blocks) :]
        for n in range(len(blocks) // 2):
            total = refs[2 * n][...].astype(F32) + refs[2 * n + 1][...].astype(F32)
            if split:
                half = total.shape[0] // 2
                outs[2 * n][...] = total[:half].astype(BF)
                outs[2 * n + 1][...] = total[half:].astype(BF)
            else:
                outs[n][...] = total.astype(BF)

    out = []
    for b in blocks[::2]:
        out += [like(b.shape[0] // 2, b.shape[1])] * 2 if split else [like(*b.shape)]
    return call(kernel, out, *blocks, after=after)


def hidden_of_lanes(core, x, zh, y):
    row = jnp.arange(512, dtype=jnp.int32)
    at = functools.partial(turned, core)
    a = (at(zh, row >> 3) * 4 + at(y, row >> 5)) * 64 + at(x, row >> 7) * 4
    b = (at(zh, row >> 3) * 4 + at(y, row >> 7)) * 64 + at(x, row >> 5) * 4 + 16
    return jnp.concatenate([a, b]) + core * 32 + jnp.concatenate([row, row]) % 4


def hidden_work(pieces, picked, cots, scale, after=()):
    rows, width = picked.shape

    def kernel(*refs):
        picked_ref, scale_ref = refs[:2]
        inner = refs[2:]
        pre_ref = refs[-1]
        for n in range(len(pieces)):
            piece, cot = inner[2 * n], inner[2 * n + 1]
            act, grad = inner[2 * len(pieces) + 2 * n :][:2]
            is_gate = lax.broadcasted_iota(jnp.int32, (1, 256), 1) & 4 == 0
            pre_ref[...] = lax.dot_general(
                picked_ref[...],
                piece[...],
                (((1,), (1,)), ((), ())),
                preferred_element_type=F32,
            )
            for r in range(0, rows, 128):
                here = pl.ds(r, 128)
                pre = pre_ref[here, :]
                gate, upval = pre, pltpu.roll(pre, 252, 1)
                weight = scale_ref[here, :]
                sigma = jax.nn.sigmoid(gate)
                act[here, :] = jnp.where(is_gate, weight * gate * sigma * upval, 0.0).astype(BF)
                scaled = cot[here, :].astype(F32) * weight
                up_grad = scaled * gate * sigma
                gate_grad = scaled * upval * sigma * (1.0 + gate * (1.0 - sigma))
                both = jnp.where(is_gate, gate_grad, pltpu.roll(up_grad, 4, 1))
                grad[here, :] = both.astype(BF)

    args = [v for pair in zip(pieces, cots) for v in pair]
    out = [like(rows, 256)] * (2 * len(pieces))
    flops = 2 * rows * 256 * width * len(pieces)
    scratch = [pltpu.VMEM((rows, 256), F32)]
    out = call(kernel, out, picked, scale, *args, after=after, flops=flops, scratch=scratch)
    return out[::2], out[1::2]


def chosen(names_ref, count):
    token = lax.broadcasted_iota(jnp.int32, (count, names_ref.shape[1]), 0)
    return (token == names_ref[...]).astype(F32).astype(BF)


def pick_rows(tokens, names, after=()):
    def kernel(tokens_ref, names_ref, out_ref):
        choice = chosen(names_ref, tokens.shape[0])
        for column in range(0, tokens.shape[1], 512):
            here = pl.ds(column, 512)
            out_ref[:, here] = lax.dot_general(
                choice,
                tokens_ref[:, here],
                (((0,), (0,)), ((), ())),
                preferred_element_type=F32,
            ).astype(BF)

    flops = 2 * tokens.size * names.shape[1]
    (out,) = call(
        kernel, [like(names.shape[1], tokens.shape[1])], tokens, names, after=after, flops=flops
    )
    return out


def slot_part(grads, pieces, first, count, arrived=None, names=None, tokens=0, after=()):
    width = pieces[0].shape[1]
    extra = [] if arrived is None else [arrived, names]

    def kernel(*refs):
        out = refs[-1]
        if extra:
            choice = chosen(refs[9], tokens)
        for column in range(0, width, 512):
            here = pl.ds(column, 512)
            part = 0.0
            for n in range(4):
                part += jnp.dot(
                    refs[n][pl.ds(first, count), :],
                    refs[4 + n][:, here],
                    preferred_element_type=F32,
                )
            if extra:
                total = (part + refs[8][:, here].astype(F32)).astype(BF)
                part = jnp.dot(choice, total, preferred_element_type=F32)
            out[:, here] = part.astype(BF)

    flops = 2 * count * 1024 * width
    (out,) = call(
        kernel,
        [like(tokens or count, width)],
        *grads,
        *pieces,
        *extra,
        after=after,
        flops=flops,
    )
    return out


def weight_part(grads, picked, factor, after=()):
    width = picked.shape[1]

    def kernel(picked_ref, *refs):
        for n in range(len(grads)):
            for column in range(0, width, 512):
                here = pl.ds(column, 512)
                part = lax.dot_general(
                    refs[n][...],
                    picked_ref[:, here],
                    (((0,), (0,)), ((), ())),
                    preferred_element_type=F32,
                )
                refs[len(grads) + n][:, here] = (part * factor).astype(BF)

    flops = 2 * picked.size * 256 * len(grads)
    return call(
        kernel, [like(256, width)] * len(grads), picked, *grads, after=after, flops=flops
    )


def local(tokens, slot_tokens, slot_counts, route_weight, cotangent, weights):
    core, x = lax.axis_index("c"), lax.axis_index("x")
    zh, y = lax.axis_index("zh"), lax.axis_index("y")
    slots = slot_tokens.shape[0]
    width = tokens.shape[1]
    factor = 1.0 / (slots * 256) ** 0.5

    row = jnp.arange(16, dtype=jnp.int32)
    group = jnp.where(row < 8, x, 4 + x)
    wanted = ((row >> 2) & 1) * 64 + core * 32 + group * 4 + row % 4
    choose = (wanted[:, None] == jnp.arange(128, dtype=jnp.int32)[None]).astype(BF)
    own = jnp.dot(choose, weights.reshape(128, width), preferred_element_type=F32).astype(BF)

    names = slot_tokens.reshape(1, slots)
    used = (jnp.arange(slots, dtype=jnp.int32) < slot_counts[0]).astype(F32)
    scale_own = (route_weight * used).reshape(2, 128)

    (own,) = join(own, swap(own, "zh", 0))
    picked_own = pick_rows(tokens, names, after=[own])
    picked_other = swap(picked_own, "c")
    a, b = join_parts(own, swap(own, "zh", 1))
    cot_other = swap(cotangent, "c")
    scale_other = swap(scale_own, "c")
    a, b = join(a, swap(a, "y", 0), b, swap(b, "x", 0), after=[picked_other])
    a, b = join(a, swap(a, "y", 1), b, swap(b, "x", 1), after=[cot_other, scale_other])
    a, b = join(a, swap(a, "x", 0), b, swap(b, "y", 0))
    a_new, b_new = swap(a, "x", 1), swap(b, "y", 1)

    picked = jnp.concatenate([picked_own, picked_other], axis=0)
    scale = jnp.concatenate([scale_own, scale_other], axis=0).reshape(2 * slots, 1)
    lanes = lax.optimization_barrier(hidden_of_lanes(core, x, zh, y))
    lanes_other = lax.optimization_barrier(hidden_of_lanes(1 - core, x, zh, y))
    hidden = jnp.arange(1024, dtype=jnp.int32)
    spread = (hidden[:, None] == lanes[None]).astype(BF)
    cot = jnp.dot(
        jnp.concatenate([cotangent, cot_other], axis=0), spread, preferred_element_type=F32
    ).astype(BF)
    cots = [cot[:, 256 * n : 256 * (n + 1)] for n in range(4)]

    acts_old, grads_old = hidden_work([a, b], picked, cots[::2], scale)
    acts_new, grads_new = hidden_work([a_new, b_new], picked, cots[1::2], scale, after=acts_old)

    a_send, b_send = weight_part(grads_new, picked, factor)
    a_in, b_in = swap(a_send, "x", 1), swap(b_send, "y", 1)
    a_own, b_own = weight_part(grads_old, picked, factor)
    grads = [grads_old[0], grads_new[0], grads_old[1], grads_new[1]]
    pieces = [a, a_new, b, b_new]
    act = jnp.concatenate([acts_old[0], acts_new[0], acts_old[1], acts_new[1]], axis=1)
    act_other = swap(act[slots:], "c")
    grad_other = swap(slot_part(grads, pieces, slots, slots, after=[a_send]), "c")
    a_own, a_send, b_own, b_send = add(a_own, a_in, b_own, b_in, after=[act_other])

    gate_lane = (jnp.arange(1024, dtype=jnp.int32) & 4 == 0)[:, None]
    back = ((hidden[None] == lanes[:, None]) & gate_lane).astype(BF)
    back_other = ((hidden[None] == lanes_other[:, None]) & gate_lane).astype(BF)
    activation = (
        jnp.dot(act[:slots], back, preferred_element_type=F32)
        + jnp.dot(act_other, back_other, preferred_element_type=F32)
    ).astype(BF)
    token_grad = slot_part(
        grads, pieces, 0, slots, grad_other, names, tokens.shape[0], after=[a_own]
    )

    a_in, b_in = swap(a_send, "x", 0), swap(b_send, "y", 0)
    a_own, a_send, b_own, b_send = add(a_own, a_in, b_own, b_in, after=[grad_other])
    a_in, b_in = swap(a_send, "y", 1), swap(b_send, "x", 1)
    a_own, a_send, b_own, b_send = add(a_own, a_in, b_own, b_in, after=[token_grad])
    a_in, b_in = swap(a_send, "y", 0), swap(b_send, "x", 0)
    own, send = add_parts(a_own, a_in, b_own, b_in, after=[activation])
    own, send = add(own, swap(send, "zh", 1))
    (total,) = add(own, swap(send, "zh", 0), split=False)
    (total,) = add(total, swap(total, "zl"), split=False)
    (total,) = join(total, swap(total, "x", 0))
    (total,) = join(total, swap(total, "x", 1))
    other = swap(total, "c")
    column = jnp.arange(128, dtype=jnp.int32)
    holder = jnp.where(column < 64, core, 1 - core)
    group = ((column >> 3) & 1) * 4 + turned(holder, x, column >> 4)
    place = ((column >> 2) & 1) * 64 + holder * 32 + group * 4 + column % 4
    choose = (jnp.arange(128, dtype=jnp.int32)[:, None] == place[None]).astype(BF)
    weight_grad = jnp.dot(
        choose, jnp.concatenate([total, other], axis=0), preferred_element_type=F32
    ).reshape(2, 64, width)
    return activation, token_grad, weight_grad


def solution(mesh):
    fine = Mesh(mesh.devices.reshape(SIZES), AXES)
    rows = P(AXES, None)
    panel = P(None, ("zh", "y"), None)
    return jax.shard_map(
        local,
        mesh=fine,
        in_specs=(rows, P(AXES), P(AXES), P(AXES), rows, panel),
        out_specs=(rows, rows, panel),
        check_vma=False,
    )
```

```python
import functools

import jax
import jax.numpy as jnp
import numpy as np
from jax import lax
from jax.experimental import pallas as pl
from jax.experimental.pallas import tpu as pltpu
from jax.sharding import Mesh
from jax.sharding import PartitionSpec as P

AXES = ("zl", "x", "c", "zh", "y")
SIZES = (2, 4, 2, 4, 4)
MASKS = ((1, 3), (3, 1))
BF = jnp.bfloat16
F32 = jnp.float32
VMEM = pl.BlockSpec(memory_space=pltpu.VMEM)
ANY = pl.BlockSpec(memory_space=pl.ANY)


def pairs(axis, stage):
    index = np.arange(256).reshape(SIZES)
    out = []
    for source in range(256):
        place = list(np.unravel_index(source, SIZES))
        at = AXES.index(axis)
        place[at] ^= MASKS[place[2]][stage] if SIZES[at] == 4 else 1
        out.append((source, int(index[tuple(place)])))
    return out


def swap(value, axis, stage=0):
    return lax.ppermute(value, AXES, pairs(axis, stage))


def mask_of(core, stage):
    return jnp.where(core == 0, MASKS[0][stage], MASKS[1][stage])


def turned(core, place, index):
    place = place ^ jnp.where(index & 1 != 0, mask_of(core, 0), 0)
    return place ^ jnp.where(index & 2 != 0, mask_of(core, 1), 0)


def call(kernel, out, *args, after=(), flops=0, scratch=(), room=2**21):
    size = sum(a.size * a.dtype.itemsize for a in (*args, *out))

    def body(*refs):
        refs = refs[: len(args)] + refs[len(args) + len(after) :]
        kernel(*refs)

    return pl.pallas_call(
        body,
        out_shape=out,
        in_specs=[VMEM] * len(args) + [ANY] * len(after),
        out_specs=[VMEM] * len(out),
        scratch_shapes=scratch,
        compiler_params=pltpu.CompilerParams(vmem_limit_bytes=size + room),
        cost_estimate=pl.CostEstimate(flops=0, bytes_accessed=1, transcendentals=0),
    )(*args, *after)


def like(rows, width, dtype=BF):
    return jax.ShapeDtypeStruct((rows, width), dtype)


def join(*blocks, after=()):
    def kernel(*refs):
        for n in range(len(blocks) // 2):
            one, two = refs[2 * n], refs[2 * n + 1]
            out = refs[len(blocks) + n]
            if one.shape[0] % 16:
                both = jnp.concatenate([one[...].astype(F32), two[...].astype(F32)], axis=0)
                out[...] = both.astype(BF)
            else:
                out[: one.shape[0]] = one[...]
                out[one.shape[0] :] = two[...]

    out = [like(2 * b.shape[0], b.shape[1]) for b in blocks[::2]]
    return call(kernel, out, *blocks, after=after)


def halves_by_part(both):
    blocks = [both[n : n + 8] for n in range(0, both.shape[0], 8)]
    return jnp.concatenate(blocks[::2], axis=0), jnp.concatenate(blocks[1::2], axis=0)


def join_parts(one, two, after=()):
    def kernel(one_ref, two_ref, a_ref, b_ref):
        both = jnp.concatenate([one_ref[...].astype(F32), two_ref[...].astype(F32)], axis=0)
        a, b = halves_by_part(both)
        a_ref[...] = a.astype(BF)
        b_ref[...] = b.astype(BF)

    return call(kernel, [like(*one.shape)] * 2, one, two, after=after)


def add_parts(a, a_in, b, b_in, after=()):
    def kernel(a_ref, a_in_ref, b_ref, b_in_ref, own_ref, send_ref):
        sum_a = a_ref[...].astype(F32) + a_in_ref[...].astype(F32)
        sum_b = b_ref[...].astype(F32) + b_in_ref[...].astype(F32)
        blocks = []
        for n in range(0, sum_a.shape[0], 8):
            blocks += [sum_a[n : n + 8], sum_b[n : n + 8]]
        half = len(blocks) // 2
        own_ref[...] = jnp.concatenate(blocks[:half], axis=0).astype(BF)
        send_ref[...] = jnp.concatenate(blocks[half:], axis=0).astype(BF)

    return call(kernel, [like(*a.shape)] * 2, a, a_in, b, b_in, after=after)


def add(*groups, split=True, after=()):
    blocks = [b for group in groups for b in group]

    def kernel(*refs):
        ins, outs = list(refs[: len(blocks)]), list(refs[len(blocks) :])
        for group in groups:
            total = sum(ins.pop(0)[...].astype(F32) for _ in group)
            if split:
                half = total.shape[0] // 2
                outs.pop(0)[...] = total[:half].astype(BF)
                outs.pop(0)[...] = total[half:].astype(BF)
            else:
                outs.pop(0)[...] = total.astype(BF)

    out = []
    for b, *_ in groups:
        out += [like(b.shape[0] // 2, b.shape[1])] * 2 if split else [like(*b.shape)]
    return call(kernel, out, *blocks, after=after)


def hidden_of_lanes(core, x, zh, y):
    row = jnp.arange(512, dtype=jnp.int32)
    at = functools.partial(turned, core)
    a = (at(zh, row >> 3) * 4 + at(y, row >> 5)) * 64 + at(x, row >> 7) * 4
    b = (at(zh, row >> 3) * 4 + at(y, row >> 7)) * 64 + at(x, row >> 5) * 4 + 16
    both = jnp.stack([a.reshape(4, 128), b.reshape(4, 128)], axis=1).reshape(1024)
    return both + core * 32 + jnp.concatenate([row, row]) % 4


def hidden_work(blocks, picked, cots, scale, after=()):
    rows, width = picked.shape
    count = len(blocks)

    def kernel(*refs):
        picked_ref, scale_ref = refs[:2]
        pre_ref = refs[-1]
        for n in range(count):
            a_ref, b_ref, cot = refs[2 + 3 * n : 5 + 3 * n]
            act, grad = refs[2 + 3 * count + 2 * n :][:2]
            is_gate = lax.broadcasted_iota(jnp.int32, (1, 256), 1) & 4 == 0
            pre_ref[...] = lax.dot_general(
                picked_ref[...],
                jnp.concatenate([a_ref[...], b_ref[...]], axis=0),
                (((1,), (1,)), ((), ())),
                preferred_element_type=F32,
            )
            for r in range(0, rows, 128):
                here = pl.ds(r, 128)
                pre = pre_ref[here, :]
                gate, upval = pre, pltpu.roll(pre, 252, 1)
                weight = scale_ref[here, :]
                sigma = jax.nn.sigmoid(gate)
                act[here, :] = jnp.where(is_gate, weight * gate * sigma * upval, 0.0).astype(BF)
                scaled = cot[here, :].astype(F32) * weight
                up_grad = scaled * gate * sigma
                gate_grad = scaled * upval * sigma * (1.0 + gate * (1.0 - sigma))
                both = jnp.where(is_gate, gate_grad, pltpu.roll(up_grad, 4, 1))
                grad[here, :] = both.astype(BF)

    args = [v for (a, b), cot in zip(blocks, cots) for v in (a, b, cot)]
    out = [like(rows, 256)] * (2 * count)
    flops = 2 * rows * 256 * width * count
    scratch = [pltpu.VMEM((rows, 256), F32)]
    out = call(kernel, out, picked, scale, *args, after=after, flops=flops, scratch=scratch, room=6 * 2**20)
    return out[::2], out[1::2]


def chosen(names_ref, count):
    token = lax.broadcasted_iota(jnp.int32, (count, names_ref.shape[1]), 0)
    return (token == names_ref[...]).astype(F32).astype(BF)


def pick_rows(tokens, names, after=()):
    def kernel(tokens_ref, names_ref, out_ref):
        choice = chosen(names_ref, tokens.shape[0])
        for column in range(0, tokens.shape[1], 512):
            here = pl.ds(column, 512)
            out_ref[:, here] = lax.dot_general(
                choice,
                tokens_ref[:, here],
                (((0,), (0,)), ((), ())),
                preferred_element_type=F32,
            ).astype(BF)

    flops = 2 * tokens.size * names.shape[1]
    (out,) = call(
        kernel, [like(names.shape[1], tokens.shape[1])], tokens, names, after=after, flops=flops, room=2**22
    )
    return out


def slot_part(grads, pieces, first, count, arrived=None, names=None, tokens=0, after=()):
    width = pieces[0].shape[1]
    extra = [] if arrived is None else [arrived, names]

    def kernel(*refs):
        out = refs[-1]
        if extra:
            choice = chosen(refs[13], tokens)
        for column in range(0, width, 512):
            here = pl.ds(column, 512)
            part = 0.0
            for n in range(4):
                a_ref, b_ref = refs[4 + 2 * n : 6 + 2 * n]
                part += jnp.dot(
                    refs[n][pl.ds(first, count), :],
                    jnp.concatenate([a_ref[:, here], b_ref[:, here]], axis=0),
                    preferred_element_type=F32,
                )
            if extra:
                total = (part + refs[12][:, here].astype(F32)).astype(BF)
                part = jnp.dot(choice, total, preferred_element_type=F32)
            out[:, here] = part.astype(BF)

    flops = 2 * count * 1024 * width
    (out,) = call(
        kernel,
        [like(tokens or count, width)],
        *grads,
        *pieces,
        *extra,
        after=after,
        flops=flops,
        room=6 * 2**20,
    )
    return out


def weight_part(grads, picked, factor, after=()):
    width = picked.shape[1]

    def kernel(picked_ref, *refs):
        for n in range(len(grads)):
            a_ref, b_ref = refs[len(grads) + 2 * n :][:2]
            for column in range(0, width, 512):
                here = pl.ds(column, 512)
                part = lax.dot_general(
                    refs[n][...],
                    picked_ref[:, here],
                    (((0,), (0,)), ((), ())),
                    preferred_element_type=F32,
                )
                a_ref[:, here] = (part[:128] * factor).astype(BF)
                b_ref[:, here] = (part[128:] * factor).astype(BF)

    flops = 2 * picked.size * 256 * len(grads)
    out = [like(128, width)] * (2 * len(grads))
    return call(kernel, out, picked, *grads, after=after, flops=flops, room=6 * 2**20)


def local(tokens, slot_tokens, slot_counts, route_weight, cotangent, weights):
    core, x = lax.axis_index("c"), lax.axis_index("x")
    zh, y = lax.axis_index("zh"), lax.axis_index("y")
    slots = slot_tokens.shape[0]
    width = tokens.shape[1]
    factor = 1.0 / (slots * 256) ** 0.5

    row = jnp.arange(16, dtype=jnp.int32)
    group = jnp.where(row < 8, x, 4 + x)
    wanted = ((row >> 2) & 1) * 64 + core * 32 + group * 4 + row % 4
    choose = (wanted[:, None] == jnp.arange(128, dtype=jnp.int32)[None]).astype(BF)
    own = jnp.dot(choose, weights.reshape(128, width), preferred_element_type=F32).astype(BF)

    names = slot_tokens.reshape(1, slots)
    used = (jnp.arange(slots, dtype=jnp.int32) < slot_counts[0]).astype(F32)
    scale_own = (route_weight * used).reshape(2, 128)

    cot_other = swap(cotangent, "c")
    scale_other = swap(scale_own, "c")
    picked_own = pick_rows(tokens, names, after=[own])
    (own,) = join(own, swap(own, "zh", 0), after=[picked_own])
    a, b = join_parts(own, swap(own, "zh", 1), after=[cot_other, scale_other])
    picked_other = swap(picked_own, "c")
    a, b = join(a, swap(a, "y", 0), b, swap(b, "x", 0))
    a, b = join(a, swap(a, "y", 1), b, swap(b, "x", 1))
    a1, b1, a2, b2 = swap(a, "x", 0), swap(b, "y", 0), swap(a, "x", 1), swap(b, "y", 1)
    a3, b3 = swap(a1, "x", 1), swap(b1, "y", 1)

    picked = jnp.concatenate([picked_own, picked_other], axis=0)
    scale = jnp.concatenate([scale_own, scale_other], axis=0).reshape(2 * slots, 1)
    lanes = lax.optimization_barrier(hidden_of_lanes(core, x, zh, y))
    lanes_other = lax.optimization_barrier(hidden_of_lanes(1 - core, x, zh, y))
    hidden = jnp.arange(1024, dtype=jnp.int32)
    spread = (hidden[:, None] == lanes[None]).astype(BF)
    cot = jnp.dot(
        jnp.concatenate([cotangent, cot_other], axis=0), spread, preferred_element_type=F32
    ).astype(BF)
    cots = [cot[:, 256 * n : 256 * (n + 1)] for n in range(4)]

    acts0, grads0 = hidden_work([(a, b)], picked, cots[:1], scale)
    acts1, grads1 = hidden_work([(a1, b1), (a2, b2)], picked, cots[1:3], scale, after=acts0)
    a_own, b_own = weight_part(grads0, picked, factor)
    a_mid, b_mid, a_near, b_near = weight_part(grads1, picked, factor)
    acts3, grads3 = hidden_work([(a3, b3)], picked, cots[3:], scale, after=[a_own, a_near])
    acts = [*acts0, *acts1, *acts3]
    grads = [*grads0, *grads1, *grads3]
    pieces = [a, b, a1, b1, a2, b2, a3, b3]

    a_far, b_far = weight_part(grads3, picked, factor)
    a_in, b_in = swap(a_far, "x", 1), swap(b_far, "y", 1)
    a_direct, b_direct = swap(a_near, "x", 1), swap(b_near, "y", 1)
    a_mid, b_mid = add(
        [a_mid, a_in], [b_mid, b_in], split=False, after=[a_direct, b_direct]
    )
    grad_other = swap(slot_part(grads, pieces, slots, slots, after=[a_mid]), "c")
    act = jnp.concatenate(acts, axis=1)
    act_other = swap(act[slots:], "c")

    gate_lane = (jnp.arange(1024, dtype=jnp.int32) & 4 == 0)[:, None]
    back = ((hidden[None] == lanes[:, None]) & gate_lane).astype(BF)
    back_other = ((hidden[None] == lanes_other[:, None]) & gate_lane).astype(BF)
    activation = (
        jnp.dot(act[:slots], back, preferred_element_type=F32)
        + jnp.dot(act_other, back_other, preferred_element_type=F32)
    ).astype(BF)
    token_grad = slot_part(
        grads, pieces, 0, slots, grad_other, names, tokens.shape[0], after=[a_mid]
    )

    a_in, b_in = swap(a_mid, "x", 0), swap(b_mid, "y", 0)
    a_own, a_send, b_own, b_send = add([a_own, a_direct, a_in], [b_own, b_direct, b_in])
    a_in, b_in = swap(a_send, "y", 1), swap(b_send, "x", 1)
    a_own, a_send, b_own, b_send = add([a_own, a_in], [b_own, b_in])
    a_in, b_in = swap(a_send, "y", 0), swap(b_send, "x", 0)
    own, send = add_parts(a_own, a_in, b_own, b_in)
    own, send = add([own, swap(send, "zh", 1)], after=[token_grad])
    (total,) = add([own, swap(send, "zh", 0)], split=False, after=[activation])
    (total,) = add([total, swap(total, "zl")], split=False)
    (total,) = join(total, swap(total, "x", 0))
    (total,) = join(total, swap(total, "x", 1))
    other = swap(total, "c")
    column = jnp.arange(128, dtype=jnp.int32)
    holder = jnp.where(column < 64, core, 1 - core)
    group = ((column >> 3) & 1) * 4 + turned(holder, x, column >> 4)
    place = ((column >> 2) & 1) * 64 + holder * 32 + group * 4 + column % 4
    choose = (jnp.arange(128, dtype=jnp.int32)[:, None] == place[None]).astype(BF)
    weight_grad = jnp.dot(
        choose, jnp.concatenate([total, other], axis=0), preferred_element_type=F32
    ).reshape(2, 64, width)
    return activation, token_grad, weight_grad


def solution(mesh):
    fine = Mesh(mesh.devices.reshape(SIZES), AXES)
    rows = P(AXES, None)
    panel = P(None, ("zh", "y"), None)
    return jax.shard_map(
        local,
        mesh=fine,
        in_specs=(rows, P(AXES), P(AXES), P(AXES), rows, panel),
        out_specs=(rows, rows, panel),
        check_vma=False,
    )
```

```python
import functools

import jax
import jax.numpy as jnp
import numpy as np
from jax import lax
from jax.experimental import pallas as pl
from jax.experimental.pallas import tpu as pltpu
from jax.sharding import Mesh
from jax.sharding import PartitionSpec as P

AXES = ("zl", "x", "c", "zh", "y")
SIZES = (2, 4, 2, 4, 4)
MASKS = ((1, 3), (3, 1))
BF = jnp.bfloat16
F32 = jnp.float32
VMEM = pl.BlockSpec(memory_space=pltpu.VMEM)
ANY = pl.BlockSpec(memory_space=pl.ANY)


def pairs(axis, stage):
    index = np.arange(256).reshape(SIZES)
    out = []
    for source in range(256):
        place = list(np.unravel_index(source, SIZES))
        at = AXES.index(axis)
        place[at] ^= MASKS[place[2]][stage] if SIZES[at] == 4 else 1
        out.append((source, int(index[tuple(place)])))
    return out


def swap(value, axis, stage=0):
    return lax.ppermute(value, AXES, pairs(axis, stage))


def mask_of(core, stage):
    return jnp.where(core == 0, MASKS[0][stage], MASKS[1][stage])


def turned(core, place, index):
    place = place ^ jnp.where(index & 1 != 0, mask_of(core, 0), 0)
    return place ^ jnp.where(index & 2 != 0, mask_of(core, 1), 0)


def call(kernel, out, *args, after=(), flops=0, scratch=(), room=2**21):
    size = sum(a.size * a.dtype.itemsize for a in (*args, *out))

    def body(*refs):
        refs = refs[: len(args)] + refs[len(args) + len(after) :]
        kernel(*refs)

    return pl.pallas_call(
        body,
        out_shape=out,
        in_specs=[VMEM] * len(args) + [ANY] * len(after),
        out_specs=[VMEM] * len(out),
        scratch_shapes=scratch,
        compiler_params=pltpu.CompilerParams(vmem_limit_bytes=size + room),
        cost_estimate=pl.CostEstimate(flops=0, bytes_accessed=1, transcendentals=0),
    )(*args, *after)


def like(rows, width, dtype=BF):
    return jax.ShapeDtypeStruct((rows, width), dtype)


def join(*blocks, after=()):
    def kernel(*refs):
        for n in range(len(blocks) // 2):
            one, two = refs[2 * n], refs[2 * n + 1]
            out = refs[len(blocks) + n]
            if one.shape[0] % 16:
                both = jnp.concatenate([one[...].astype(F32), two[...].astype(F32)], axis=0)
                out[...] = both.astype(BF)
            else:
                out[: one.shape[0]] = one[...]
                out[one.shape[0] :] = two[...]

    out = [like(2 * b.shape[0], b.shape[1]) for b in blocks[::2]]
    return call(kernel, out, *blocks, after=after)


def halves_by_part(both):
    blocks = [both[n : n + 8] for n in range(0, both.shape[0], 8)]
    return jnp.concatenate(blocks[::2], axis=0), jnp.concatenate(blocks[1::2], axis=0)


def join_parts(one, two, after=()):
    def kernel(one_ref, two_ref, a_ref, b_ref):
        both = jnp.concatenate([one_ref[...].astype(F32), two_ref[...].astype(F32)], axis=0)
        a, b = halves_by_part(both)
        a_ref[...] = a.astype(BF)
        b_ref[...] = b.astype(BF)

    return call(kernel, [like(*one.shape)] * 2, one, two, after=after)


def add_parts(a, a_in, b, b_in, after=()):
    def kernel(a_ref, a_in_ref, b_ref, b_in_ref, own_ref, send_ref):
        sum_a = a_ref[...].astype(F32) + a_in_ref[...].astype(F32)
        sum_b = b_ref[...].astype(F32) + b_in_ref[...].astype(F32)
        blocks = []
        for n in range(0, sum_a.shape[0], 8):
            blocks += [sum_a[n : n + 8], sum_b[n : n + 8]]
        half = len(blocks) // 2
        own_ref[...] = jnp.concatenate(blocks[:half], axis=0).astype(BF)
        send_ref[...] = jnp.concatenate(blocks[half:], axis=0).astype(BF)

    return call(kernel, [like(*a.shape)] * 2, a, a_in, b, b_in, after=after)


def add(*groups, split=True, after=()):
    blocks = [b for group in groups for b in group]

    def kernel(*refs):
        ins, outs = list(refs[: len(blocks)]), list(refs[len(blocks) :])
        for group in groups:
            total = sum(ins.pop(0)[...].astype(F32) for _ in group)
            if split:
                half = total.shape[0] // 2
                outs.pop(0)[...] = total[:half].astype(BF)
                outs.pop(0)[...] = total[half:].astype(BF)
            else:
                outs.pop(0)[...] = total.astype(BF)

    out = []
    for b, *_ in groups:
        out += [like(b.shape[0] // 2, b.shape[1])] * 2 if split else [like(*b.shape)]
    return call(kernel, out, *blocks, after=after)


def hidden_of_lanes(core, x, zh, y):
    row = jnp.arange(512, dtype=jnp.int32)
    at = functools.partial(turned, core)
    a = (at(zh, row >> 3) * 4 + at(y, row >> 5)) * 64 + at(x, row >> 7) * 4
    b = (at(zh, row >> 3) * 4 + at(y, row >> 7)) * 64 + at(x, row >> 5) * 4 + 16
    both = jnp.stack([a.reshape(4, 128), b.reshape(4, 128)], axis=1).reshape(1024)
    return both + core * 32 + jnp.concatenate([row, row]) % 4


def hidden_work(blocks, picked, cots, scale, after=()):
    rows, width = picked.shape
    count = len(blocks)

    def kernel(*refs):
        picked_ref, scale_ref = refs[:2]
        pre_ref = refs[-1]
        for n in range(count):
            a_ref, b_ref, cot = refs[2 + 3 * n : 5 + 3 * n]
            act, grad = refs[2 + 3 * count + 2 * n :][:2]
            is_gate = lax.broadcasted_iota(jnp.int32, (1, 256), 1) & 4 == 0
            pre_ref[...] = lax.dot_general(
                picked_ref[...],
                jnp.concatenate([a_ref[...], b_ref[...]], axis=0),
                (((1,), (1,)), ((), ())),
                preferred_element_type=F32,
            )
            for r in range(0, rows, 128):
                here = pl.ds(r, 128)
                pre = pre_ref[here, :]
                gate, upval = pre, pltpu.roll(pre, 252, 1)
                weight = scale_ref[here, :]
                sigma = jax.nn.sigmoid(gate)
                act[here, :] = jnp.where(is_gate, weight * gate * sigma * upval, 0.0).astype(BF)
                scaled = cot[here, :].astype(F32) * weight
                up_grad = scaled * gate * sigma
                gate_grad = scaled * upval * sigma * (1.0 + gate * (1.0 - sigma))
                both = jnp.where(is_gate, gate_grad, pltpu.roll(up_grad, 4, 1))
                grad[here, :] = both.astype(BF)

    args = [v for (a, b), cot in zip(blocks, cots) for v in (a, b, cot)]
    out = [like(rows, 256)] * (2 * count)
    flops = 2 * rows * 256 * width * count
    scratch = [pltpu.VMEM((rows, 256), F32)]
    out = call(kernel, out, picked, scale, *args, after=after, flops=flops, scratch=scratch, room=6 * 2**20)
    return out[::2], out[1::2]


def chosen(names_ref, count):
    token = lax.broadcasted_iota(jnp.int32, (count, names_ref.shape[1]), 0)
    return (token == names_ref[...]).astype(F32).astype(BF)


def pick_rows(tokens, names, after=()):
    def kernel(tokens_ref, names_ref, out_ref):
        choice = chosen(names_ref, tokens.shape[0])
        for column in range(0, tokens.shape[1], 512):
            here = pl.ds(column, 512)
            out_ref[:, here] = lax.dot_general(
                choice,
                tokens_ref[:, here],
                (((0,), (0,)), ((), ())),
                preferred_element_type=F32,
            ).astype(BF)

    flops = 2 * tokens.size * names.shape[1]
    (out,) = call(
        kernel, [like(names.shape[1], tokens.shape[1])], tokens, names, after=after, flops=flops, room=2**22
    )
    return out


def slot_part(grads, pieces, count, after=()):
    width = pieces[0].shape[1]

    def kernel(*refs):
        own_ref, other_ref = refs[12:]
        for column in range(0, width, 512):
            here = pl.ds(column, 512)
            part = 0.0
            for n in range(4):
                a_ref, b_ref = refs[4 + 2 * n : 6 + 2 * n]
                part += jnp.dot(
                    refs[n][...],
                    jnp.concatenate([a_ref[:, here], b_ref[:, here]], axis=0),
                    preferred_element_type=F32,
                )
            own_ref[:, here] = part[:count]
            other_ref[:, here] = part[count:].astype(BF)

    out = [like(count, width, F32), like(count, width)]
    return call(kernel, out, *grads, *pieces, after=after, room=6 * 2**20)


def to_tokens(own, arrived, names, tokens, after=()):
    width = own.shape[1]

    def kernel(own_ref, arrived_ref, names_ref, out):
        choice = chosen(names_ref, tokens)
        for column in range(0, width, 512):
            here = pl.ds(column, 512)
            total = (own_ref[:, here] + arrived_ref[:, here].astype(F32)).astype(BF)
            part = jnp.dot(choice, total, preferred_element_type=F32)
            out[:, here] = part.astype(BF)

    (out,) = call(
        kernel, [like(tokens, width)], own, arrived, names, after=after, room=6 * 2**20
    )
    return out


def behind(blocks, after):
    count = len(blocks)
    return pl.pallas_call(
        lambda *refs: None,
        out_shape=[like(*b.shape) for b in blocks],
        in_specs=[ANY] * (count + len(after)),
        out_specs=[ANY] * count,
        input_output_aliases={n: n for n in range(count)},
        cost_estimate=pl.CostEstimate(flops=0, bytes_accessed=1, transcendentals=0),
    )(*blocks, *after)


def weight_part(grads, picked, factor, after=()):
    width = picked.shape[1]

    def kernel(picked_ref, *refs):
        for n in range(len(grads)):
            a_ref, b_ref = refs[len(grads) + 2 * n :][:2]
            for column in range(0, width, 512):
                here = pl.ds(column, 512)
                part = lax.dot_general(
                    refs[n][...],
                    picked_ref[:, here],
                    (((0,), (0,)), ((), ())),
                    preferred_element_type=F32,
                )
                a_ref[:, here] = (part[:128] * factor).astype(BF)
                b_ref[:, here] = (part[128:] * factor).astype(BF)

    flops = 2 * picked.size * 256 * len(grads)
    out = [like(128, width)] * (2 * len(grads))
    return call(kernel, out, picked, *grads, after=after, flops=flops, room=6 * 2**20)


def local(tokens, slot_tokens, slot_counts, route_weight, cotangent, weights):
    core, x = lax.axis_index("c"), lax.axis_index("x")
    zh, y = lax.axis_index("zh"), lax.axis_index("y")
    slots = slot_tokens.shape[0]
    width = tokens.shape[1]
    factor = 1.0 / (slots * 256) ** 0.5

    row = jnp.arange(16, dtype=jnp.int32)
    group = jnp.where(row < 8, x, 4 + x)
    wanted = ((row >> 2) & 1) * 64 + core * 32 + group * 4 + row % 4
    choose = (wanted[:, None] == jnp.arange(128, dtype=jnp.int32)[None]).astype(BF)
    own = jnp.dot(choose, weights.reshape(128, width), preferred_element_type=F32).astype(BF)

    names = slot_tokens.reshape(1, slots)
    used = (jnp.arange(slots, dtype=jnp.int32) < slot_counts[0]).astype(F32)
    scale_own = (route_weight * used).reshape(2, 128)

    cot_other = swap(cotangent, "c")
    scale_other = swap(scale_own, "c")
    picked_own = pick_rows(tokens, names, after=[own])
    (own,) = join(own, swap(own, "zh", 0), after=[picked_own])
    a, b = join_parts(own, swap(own, "zh", 1), after=[cot_other, scale_other])
    picked_other = swap(picked_own, "c")
    a, b = join(a, swap(a, "y", 0), b, swap(b, "x", 0))
    lanes = lax.optimization_barrier(hidden_of_lanes(core, x, zh, y))
    lanes_other = lax.optimization_barrier(hidden_of_lanes(1 - core, x, zh, y))
    hidden = jnp.arange(1024, dtype=jnp.int32)
    spread = (hidden[:, None] == lanes[None]).astype(BF)
    cot = jnp.dot(
        jnp.concatenate([cotangent, cot_other], axis=0), spread, preferred_element_type=F32
    ).astype(BF)
    cots = [cot[:, 256 * n : 256 * (n + 1)] for n in range(4)]

    a, b = join(a, swap(a, "y", 1), b, swap(b, "x", 1), after=cots)
    a1, b1, a2, b2 = swap(a, "x", 0), swap(b, "y", 0), swap(a, "x", 1), swap(b, "y", 1)

    picked = jnp.concatenate([picked_own, picked_other], axis=0)
    scale = jnp.concatenate([scale_own, scale_other], axis=0).reshape(2 * slots, 1)
    acts0, grads0 = hidden_work([(a, b)], picked, cots[:1], scale)
    a_own, b_own = weight_part(grads0, picked, factor)
    a1, b1 = behind([a1, b1], [a_own])
    a3, b3 = swap(a1, "x", 1), swap(b1, "y", 1)
    acts1, grads1 = hidden_work([(a1, b1), (a2, b2)], picked, cots[1:3], scale)
    a_mid, b_mid, a_near, b_near = weight_part(grads1, picked, factor)
    acts3, grads3 = hidden_work([(a3, b3)], picked, cots[3:], scale, after=[a_near])
    acts = [*acts0, *acts1, *acts3]
    grads = [*grads0, *grads1, *grads3]
    pieces = [a, b, a1, b1, a2, b2, a3, b3]

    a_far, b_far = weight_part(grads3, picked, factor)
    a_in, b_in = swap(a_far, "x", 1), swap(b_far, "y", 1)
    a_direct, b_direct = swap(a_near, "x", 1), swap(b_near, "y", 1)
    a_mid, b_mid = add(
        [a_mid, a_in], [b_mid, b_in], split=False
    )
    slot_own, slot_other = slot_part(grads, pieces, slots, after=[a_mid])
    grad_other = swap(slot_other, "c")
    act = jnp.concatenate(acts, axis=1)
    act_other = swap(act[slots:], "c")

    gate_lane = (jnp.arange(1024, dtype=jnp.int32) & 4 == 0)[:, None]
    back = ((hidden[None] == lanes[:, None]) & gate_lane).astype(BF)
    back_other = ((hidden[None] == lanes_other[:, None]) & gate_lane).astype(BF)
    activation = (
        jnp.dot(act[:slots], back, preferred_element_type=F32)
        + jnp.dot(act_other, back_other, preferred_element_type=F32)
    ).astype(BF)
    token_grad = to_tokens(slot_own, grad_other, names, tokens.shape[0])

    a_in, b_in = swap(a_mid, "x", 0), swap(b_mid, "y", 0)
    a_own, a_send, b_own, b_send = add([a_own, a_direct, a_in], [b_own, b_direct, b_in])
    a_in, b_in = swap(a_send, "y", 1), swap(b_send, "x", 1)
    a_own, a_send, b_own, b_send = add([a_own, a_in], [b_own, b_in])
    a_in, b_in = swap(a_send, "y", 0), swap(b_send, "x", 0)
    own, send = add_parts(a_own, a_in, b_own, b_in)
    own, send = add([own, swap(send, "zh", 1)], after=[token_grad])
    (total,) = add([own, swap(send, "zh", 0)], split=False, after=[activation])
    (total,) = add([total, swap(total, "zl")], split=False)
    (total,) = join(total, swap(total, "x", 0))
    (total,) = join(total, swap(total, "x", 1))
    other = swap(total, "c")
    column = jnp.arange(128, dtype=jnp.int32)
    holder = jnp.where(column < 64, core, 1 - core)
    group = ((column >> 3) & 1) * 4 + turned(holder, x, column >> 4)
    place = ((column >> 2) & 1) * 64 + holder * 32 + group * 4 + column % 4
    choose = (jnp.arange(128, dtype=jnp.int32)[:, None] == place[None]).astype(BF)
    weight_grad = jnp.dot(
        choose, jnp.concatenate([total, other], axis=0), preferred_element_type=F32
    ).reshape(2, 64, width)
    return activation, token_grad, weight_grad


def solution(mesh):
    fine = Mesh(mesh.devices.reshape(SIZES), AXES)
    rows = P(AXES, None)
    panel = P(None, ("zh", "y"), None)
    return jax.shard_map(
        local,
        mesh=fine,
        in_specs=(rows, P(AXES), P(AXES), P(AXES), rows, panel),
        out_specs=(rows, rows, panel),
        check_vma=False,
    )
```

```python
import functools

import jax
import jax.numpy as jnp
import numpy as np
from jax import lax
from jax.experimental import pallas as pl
from jax.experimental.pallas import tpu as pltpu
from jax.sharding import Mesh
from jax.sharding import PartitionSpec as P

AXES = ("zl", "x", "c", "zh", "y")
SIZES = (2, 4, 2, 4, 4)
MASKS = ((1, 3), (3, 1))
BF = jnp.bfloat16
F32 = jnp.float32
VMEM = pl.BlockSpec(memory_space=pltpu.VMEM)
ANY = pl.BlockSpec(memory_space=pl.ANY)


def pairs(axis, stage):
    index = np.arange(256).reshape(SIZES)
    out = []
    for source in range(256):
        place = list(np.unravel_index(source, SIZES))
        at = AXES.index(axis)
        place[at] ^= MASKS[place[2]][stage] if SIZES[at] == 4 else 1
        out.append((source, int(index[tuple(place)])))
    return out


def swap(value, axis, stage=0):
    return lax.ppermute(value, AXES, pairs(axis, stage))


def mask_of(core, stage):
    return jnp.where(core == 0, MASKS[0][stage], MASKS[1][stage])


def turned(core, place, index):
    place = place ^ jnp.where(index & 1 != 0, mask_of(core, 0), 0)
    return place ^ jnp.where(index & 2 != 0, mask_of(core, 1), 0)


def call(kernel, out, *args, after=(), flops=0, scratch=(), room=2**21):
    size = sum(a.size * a.dtype.itemsize for a in (*args, *out))

    def body(*refs):
        refs = refs[: len(args)] + refs[len(args) + len(after) :]
        kernel(*refs)

    return pl.pallas_call(
        body,
        out_shape=out,
        in_specs=[VMEM] * len(args) + [ANY] * len(after),
        out_specs=[VMEM] * len(out),
        scratch_shapes=scratch,
        compiler_params=pltpu.CompilerParams(vmem_limit_bytes=size + room),
        cost_estimate=pl.CostEstimate(flops=0, bytes_accessed=1, transcendentals=0),
    )(*args, *after)


def like(rows, width, dtype=BF):
    return jax.ShapeDtypeStruct((rows, width), dtype)


def join(*blocks, after=()):
    def kernel(*refs):
        for n in range(len(blocks) // 2):
            one, two = refs[2 * n], refs[2 * n + 1]
            out = refs[len(blocks) + n]
            if one.shape[0] % 16:
                both = jnp.concatenate([one[...].astype(F32), two[...].astype(F32)], axis=0)
                out[...] = both.astype(BF)
            else:
                out[: one.shape[0]] = one[...]
                out[one.shape[0] :] = two[...]

    out = [like(2 * b.shape[0], b.shape[1]) for b in blocks[::2]]
    return call(kernel, out, *blocks, after=after)


def halves_by_part(both):
    blocks = [both[n : n + 8] for n in range(0, both.shape[0], 8)]
    return jnp.concatenate(blocks[::2], axis=0), jnp.concatenate(blocks[1::2], axis=0)


def join_parts(one, two, after=()):
    def kernel(one_ref, two_ref, a_ref, b_ref):
        both = jnp.concatenate([one_ref[...].astype(F32), two_ref[...].astype(F32)], axis=0)
        a, b = halves_by_part(both)
        a_ref[...] = a.astype(BF)
        b_ref[...] = b.astype(BF)

    return call(kernel, [like(*one.shape)] * 2, one, two, after=after)


def add_parts(a, a_in, b, b_in, after=()):
    def kernel(a_ref, a_in_ref, b_ref, b_in_ref, own_ref, send_ref):
        sum_a = a_ref[...].astype(F32) + a_in_ref[...].astype(F32)
        sum_b = b_ref[...].astype(F32) + b_in_ref[...].astype(F32)
        blocks = []
        for n in range(0, sum_a.shape[0], 8):
            blocks += [sum_a[n : n + 8], sum_b[n : n + 8]]
        half = len(blocks) // 2
        own_ref[...] = jnp.concatenate(blocks[:half], axis=0).astype(BF)
        send_ref[...] = jnp.concatenate(blocks[half:], axis=0).astype(BF)

    return call(kernel, [like(*a.shape)] * 2, a, a_in, b, b_in, after=after)


def add(*groups, split=True, after=()):
    blocks = [b for group in groups for b in group]

    def kernel(*refs):
        ins, outs = list(refs[: len(blocks)]), list(refs[len(blocks) :])
        for group in groups:
            total = sum(ins.pop(0)[...].astype(F32) for _ in group)
            if split:
                half = total.shape[0] // 2
                outs.pop(0)[...] = total[:half].astype(BF)
                outs.pop(0)[...] = total[half:].astype(BF)
            else:
                outs.pop(0)[...] = total.astype(BF)

    out = []
    for b, *_ in groups:
        out += [like(b.shape[0] // 2, b.shape[1])] * 2 if split else [like(*b.shape)]
    return call(kernel, out, *blocks, after=after)


def hidden_of_lanes(core, x, zh, y):
    row = jnp.arange(512, dtype=jnp.int32)
    at = functools.partial(turned, core)
    a = (at(zh, row >> 3) * 4 + at(y, row >> 5)) * 64 + at(x, row >> 7) * 4
    b = (at(zh, row >> 3) * 4 + at(y, row >> 7)) * 64 + at(x, row >> 5) * 4 + 16
    both = jnp.stack([a.reshape(4, 128), b.reshape(4, 128)], axis=1).reshape(1024)
    return both + core * 32 + jnp.concatenate([row, row]) % 4


def hidden_work(blocks, picked, cots, scale, after=()):
    rows, width = picked.shape
    count = len(blocks)

    def kernel(*refs):
        picked_ref, scale_ref = refs[:2]
        pre_ref = refs[-1]
        for n in range(count):
            a_ref, b_ref, cot = refs[2 + 3 * n : 5 + 3 * n]
            act, grad = refs[2 + 3 * count + 2 * n :][:2]
            is_gate = lax.broadcasted_iota(jnp.int32, (1, 256), 1) & 4 == 0
            pre_ref[...] = lax.dot_general(
                picked_ref[...],
                jnp.concatenate([a_ref[...], b_ref[...]], axis=0),
                (((1,), (1,)), ((), ())),
                preferred_element_type=F32,
            )
            for r in range(0, rows, 128):
                here = pl.ds(r, 128)
                pre = pre_ref[here, :]
                gate, upval = pre, pltpu.roll(pre, 252, 1)
                weight = scale_ref[here, :]
                sigma = jax.nn.sigmoid(gate)
                act[here, :] = jnp.where(is_gate, weight * gate * sigma * upval, 0.0).astype(BF)
                scaled = cot[here, :].astype(F32) * weight
                up_grad = scaled * gate * sigma
                gate_grad = scaled * upval * sigma * (1.0 + gate * (1.0 - sigma))
                both = jnp.where(is_gate, gate_grad, pltpu.roll(up_grad, 4, 1))
                grad[here, :] = both.astype(BF)

    args = [v for (a, b), cot in zip(blocks, cots) for v in (a, b, cot)]
    out = [like(rows, 256)] * (2 * count)
    flops = 2 * rows * 256 * width * count
    scratch = [pltpu.VMEM((rows, 256), F32)]
    out = call(kernel, out, picked, scale, *args, after=after, flops=flops, scratch=scratch, room=6 * 2**20)
    return out[::2], out[1::2]


def chosen(names_ref, count):
    token = lax.broadcasted_iota(jnp.int32, (count, names_ref.shape[1]), 0)
    return (token == names_ref[...]).astype(F32).astype(BF)


def pick_rows(tokens, names, after=()):
    def kernel(tokens_ref, names_ref, out_ref):
        choice = chosen(names_ref, tokens.shape[0])
        for column in range(0, tokens.shape[1], 512):
            here = pl.ds(column, 512)
            out_ref[:, here] = lax.dot_general(
                choice,
                tokens_ref[:, here],
                (((0,), (0,)), ((), ())),
                preferred_element_type=F32,
            ).astype(BF)

    flops = 2 * tokens.size * names.shape[1]
    (out,) = call(
        kernel, [like(names.shape[1], tokens.shape[1])], tokens, names, after=after, flops=flops, room=2**22
    )
    return out


def slot_part(grads, pieces, count, after=()):
    width = pieces[0].shape[1]

    def kernel(*refs):
        own_ref, other_ref = refs[12:]
        for column in range(0, width, 512):
            here = pl.ds(column, 512)
            part = 0.0
            for n in range(4):
                a_ref, b_ref = refs[4 + 2 * n : 6 + 2 * n]
                part += jnp.dot(
                    refs[n][...],
                    jnp.concatenate([a_ref[:, here], b_ref[:, here]], axis=0),
                    preferred_element_type=F32,
                )
            own_ref[:, here] = part[:count]
            other_ref[:, here] = part[count:].astype(BF)

    out = [like(count, width, F32), like(count, width)]
    return call(kernel, out, *grads, *pieces, after=after, room=6 * 2**20)


def to_tokens(own, arrived, names, tokens, after=()):
    width = own.shape[1]

    def kernel(own_ref, arrived_ref, names_ref, out, tag):
        tag[...] = jnp.zeros(tag.shape, BF)
        choice = chosen(names_ref, tokens)
        for column in range(0, width, 512):
            here = pl.ds(column, 512)
            total = (own_ref[:, here] + arrived_ref[:, here].astype(F32)).astype(BF)
            part = jnp.dot(choice, total, preferred_element_type=F32)
            out[:, here] = part.astype(BF)

    out = [like(tokens, width), like(16, 128)]
    return call(kernel, out, own, arrived, names, after=after, room=6 * 2**20)


def behind(blocks, after):
    count = len(blocks)
    return pl.pallas_call(
        lambda *refs: None,
        out_shape=[like(*b.shape, b.dtype) for b in blocks],
        in_specs=[ANY] * (count + len(after)),
        out_specs=[ANY] * count,
        input_output_aliases={n: n for n in range(count)},
        cost_estimate=pl.CostEstimate(flops=0, bytes_accessed=1, transcendentals=0),
    )(*blocks, *after)


def weight_part(grads, picked, factor, after=()):
    width = picked.shape[1]

    def kernel(picked_ref, *refs):
        for n in range(len(grads)):
            a_ref, b_ref = refs[len(grads) + 2 * n :][:2]
            for column in range(0, width, 512):
                here = pl.ds(column, 512)
                part = lax.dot_general(
                    refs[n][...],
                    picked_ref[:, here],
                    (((0,), (0,)), ((), ())),
                    preferred_element_type=F32,
                )
                a_ref[:, here] = (part[:128] * factor).astype(BF)
                b_ref[:, here] = (part[128:] * factor).astype(BF)

    flops = 2 * picked.size * 256 * len(grads)
    out = [like(128, width)] * (2 * len(grads))
    return call(kernel, out, picked, *grads, after=after, flops=flops, room=6 * 2**20)


def local(tokens, slot_tokens, slot_counts, route_weight, cotangent, weights):
    core, x = lax.axis_index("c"), lax.axis_index("x")
    zh, y = lax.axis_index("zh"), lax.axis_index("y")
    slots = slot_tokens.shape[0]
    width = tokens.shape[1]
    factor = 1.0 / (slots * 256) ** 0.5

    row = jnp.arange(16, dtype=jnp.int32)
    group = jnp.where(row < 8, x, 4 + x)
    wanted = ((row >> 2) & 1) * 64 + core * 32 + group * 4 + row % 4
    choose = (wanted[:, None] == jnp.arange(128, dtype=jnp.int32)[None]).astype(BF)
    own = jnp.dot(choose, weights.reshape(128, width), preferred_element_type=F32).astype(BF)

    names = slot_tokens.reshape(1, slots)
    used = (jnp.arange(slots, dtype=jnp.int32) < slot_counts[0]).astype(F32)
    scale_own = (route_weight * used).reshape(2, 128)

    cot_other = swap(cotangent, "c")
    picked_own = pick_rows(tokens, names, after=[own])
    (own,) = join(own, swap(own, "zh", 0), after=[picked_own])
    a, b = join_parts(own, swap(own, "zh", 1), after=[cot_other])
    picked_other = swap(*behind([picked_own], [a]), "c")
    a, b = join(a, swap(a, "y", 0), b, swap(b, "x", 0))
    lanes = lax.optimization_barrier(hidden_of_lanes(core, x, zh, y))
    lanes_other = lax.optimization_barrier(hidden_of_lanes(1 - core, x, zh, y))
    hidden = jnp.arange(1024, dtype=jnp.int32)
    spread = (hidden[:, None] == lanes[None]).astype(BF)
    cot = jnp.dot(
        jnp.concatenate([cotangent, cot_other], axis=0), spread, preferred_element_type=F32
    ).astype(BF)
    cots = [cot[:, 256 * n : 256 * (n + 1)] for n in range(4)]

    a, b = join(a, swap(a, "y", 1), b, swap(b, "x", 1), after=cots)
    scale_other = swap(*behind([scale_own], [a]), "c")
    a, b = behind([a, b], [scale_other])
    scale = jnp.concatenate([scale_own, scale_other], axis=0).reshape(2 * slots, 1)
    a1, b1, a2, b2 = swap(a, "x", 0), swap(b, "y", 0), swap(a, "x", 1), swap(b, "y", 1)

    picked = jnp.concatenate([picked_own, picked_other], axis=0)
    acts0, grads0 = hidden_work([(a, b)], picked, cots[:1], scale)
    a_own, b_own = weight_part(grads0, picked, factor)
    a1, b1 = behind([a1, b1], [a_own])
    a3, b3 = swap(a1, "x", 1), swap(b1, "y", 1)
    acts1, grads1 = hidden_work([(a1, b1), (a2, b2)], picked, cots[1:3], scale)
    a_mid, b_mid, a_near, b_near = weight_part(grads1, picked, factor)
    acts3, grads3 = hidden_work([(a3, b3)], picked, cots[3:], scale, after=[a_near])
    acts = [*acts0, *acts1, *acts3]
    grads = [*grads0, *grads1, *grads3]
    pieces = [a, b, a1, b1, a2, b2, a3, b3]

    a_far, b_far = weight_part(grads3, picked, factor)
    a_in, b_in = swap(a_far, "x", 1), swap(b_far, "y", 1)
    a_direct, b_direct = swap(a_near, "x", 1), swap(b_near, "y", 1)
    a_mid, b_mid = add(
        [a_mid, a_in], [b_mid, b_in], split=False
    )
    slot_own, slot_other = slot_part(grads, pieces, slots, after=[a_mid])
    grad_other = swap(slot_other, "c")
    act = jnp.concatenate(acts, axis=1)
    act_other = swap(act[slots:], "c")

    gate_lane = (jnp.arange(1024, dtype=jnp.int32) & 4 == 0)[:, None]
    back = ((hidden[None] == lanes[:, None]) & gate_lane).astype(BF)
    back_other = ((hidden[None] == lanes_other[:, None]) & gate_lane).astype(BF)
    activation = (
        jnp.dot(act[:slots], back, preferred_element_type=F32)
        + jnp.dot(act_other, back_other, preferred_element_type=F32)
    ).astype(BF)
    token_grad, tag = to_tokens(slot_own, grad_other, names, tokens.shape[0])

    a_in, b_in = swap(a_mid, "x", 0), swap(b_mid, "y", 0)
    a_own, a_send, b_own, b_send = add([a_own, a_direct, a_in], [b_own, b_direct, b_in])
    a_in, b_in = swap(a_send, "y", 1), swap(b_send, "x", 1)
    a_own, a_send, b_own, b_send = add([a_own, a_in], [b_own, b_in])
    a_in, b_in = swap(a_send, "y", 0), swap(b_send, "x", 0)
    own, send = add_parts(a_own, a_in, b_own, b_in)
    own, send = add([own, swap(send, "zh", 1)], after=[tag])
    (total,) = add([own, swap(send, "zh", 0)], split=False, after=[activation])
    (total,) = add([total, swap(total, "zl")], split=False)
    (total,) = join(total, swap(total, "x", 0))
    (total,) = join(total, swap(total, "x", 1))
    other = swap(total, "c")
    column = jnp.arange(128, dtype=jnp.int32)
    holder = jnp.where(column < 64, core, 1 - core)
    group = ((column >> 3) & 1) * 4 + turned(holder, x, column >> 4)
    place = ((column >> 2) & 1) * 64 + holder * 32 + group * 4 + column % 4
    choose = (jnp.arange(128, dtype=jnp.int32)[:, None] == place[None]).astype(BF)
    weight_grad = jnp.dot(
        choose, jnp.concatenate([total, other], axis=0), preferred_element_type=F32
    ).reshape(2, 64, width)
    return activation, token_grad, weight_grad


def solution(mesh):
    fine = Mesh(mesh.devices.reshape(SIZES), AXES)
    rows = P(AXES, None)
    panel = P(None, ("zh", "y"), None)
    return jax.shard_map(
        local,
        mesh=fine,
        in_specs=(rows, P(AXES), P(AXES), P(AXES), rows, panel),
        out_specs=(rows, rows, panel),
        check_vma=False,
    )
```

```python
import functools

import jax
import jax.numpy as jnp
import numpy as np
from jax import lax
from jax.experimental import pallas as pl
from jax.experimental.pallas import tpu as pltpu
from jax.sharding import Mesh
from jax.sharding import PartitionSpec as P

AXES = ("zl", "x", "c", "zh", "y")
SIZES = (2, 4, 2, 4, 4)
MASKS = ((1, 3), (3, 1))
BF = jnp.bfloat16
F32 = jnp.float32
VMEM = pl.BlockSpec(memory_space=pltpu.VMEM)
ANY = pl.BlockSpec(memory_space=pl.ANY)


def pairs(axis, stage):
    index = np.arange(256).reshape(SIZES)
    out = []
    for source in range(256):
        place = list(np.unravel_index(source, SIZES))
        at = AXES.index(axis)
        place[at] ^= MASKS[place[2]][stage] if SIZES[at] == 4 else 1
        out.append((source, int(index[tuple(place)])))
    return out


def swap(value, axis, stage=0):
    return lax.ppermute(value, AXES, pairs(axis, stage))


def mask_of(core, stage):
    return jnp.where(core == 0, MASKS[0][stage], MASKS[1][stage])


def turned(core, place, index):
    place = place ^ jnp.where(index & 1 != 0, mask_of(core, 0), 0)
    return place ^ jnp.where(index & 2 != 0, mask_of(core, 1), 0)


def call(kernel, out, *args, after=(), flops=0, scratch=(), room=2**21):
    size = sum(a.size * a.dtype.itemsize for a in (*args, *out))

    def body(*refs):
        refs = refs[: len(args)] + refs[len(args) + len(after) :]
        kernel(*refs)

    return pl.pallas_call(
        body,
        out_shape=out,
        in_specs=[VMEM] * len(args) + [ANY] * len(after),
        out_specs=[VMEM] * len(out),
        scratch_shapes=scratch,
        compiler_params=pltpu.CompilerParams(vmem_limit_bytes=size + room),
        cost_estimate=pl.CostEstimate(flops=0, bytes_accessed=1, transcendentals=0),
    )(*args, *after)


def like(rows, width, dtype=BF):
    return jax.ShapeDtypeStruct((rows, width), dtype)


def join(*blocks, after=()):
    def kernel(*refs):
        for n in range(len(blocks) // 2):
            one, two = refs[2 * n], refs[2 * n + 1]
            out = refs[len(blocks) + n]
            if one.shape[0] % 16:
                both = jnp.concatenate([one[...].astype(F32), two[...].astype(F32)], axis=0)
                out[...] = both.astype(BF)
            else:
                out[: one.shape[0]] = one[...]
                out[one.shape[0] :] = two[...]

    out = [like(2 * b.shape[0], b.shape[1]) for b in blocks[::2]]
    return call(kernel, out, *blocks, after=after)


def halves_by_part(both):
    blocks = [both[n : n + 8] for n in range(0, both.shape[0], 8)]
    return jnp.concatenate(blocks[::2], axis=0), jnp.concatenate(blocks[1::2], axis=0)


def join_parts(one, two, after=()):
    def kernel(one_ref, two_ref, a_ref, b_ref):
        both = jnp.concatenate([one_ref[...].astype(F32), two_ref[...].astype(F32)], axis=0)
        a, b = halves_by_part(both)
        a_ref[...] = a.astype(BF)
        b_ref[...] = b.astype(BF)

    return call(kernel, [like(*one.shape)] * 2, one, two, after=after)


def add_parts(a, a_in, b, b_in, after=()):
    def kernel(a_ref, a_in_ref, b_ref, b_in_ref, own_ref, send_ref):
        sum_a = a_ref[...].astype(F32) + a_in_ref[...].astype(F32)
        sum_b = b_ref[...].astype(F32) + b_in_ref[...].astype(F32)
        blocks = []
        for n in range(0, sum_a.shape[0], 8):
            blocks += [sum_a[n : n + 8], sum_b[n : n + 8]]
        half = len(blocks) // 2
        own_ref[...] = jnp.concatenate(blocks[:half], axis=0).astype(BF)
        send_ref[...] = jnp.concatenate(blocks[half:], axis=0).astype(BF)

    return call(kernel, [like(*a.shape)] * 2, a, a_in, b, b_in, after=after)


def add(*groups, split=True, after=()):
    blocks = [b for group in groups for b in group]

    def kernel(*refs):
        ins, outs = list(refs[: len(blocks)]), list(refs[len(blocks) :])
        for group in groups:
            total = sum(ins.pop(0)[...].astype(F32) for _ in group)
            if split:
                half = total.shape[0] // 2
                outs.pop(0)[...] = total[:half].astype(BF)
                outs.pop(0)[...] = total[half:].astype(BF)
            else:
                outs.pop(0)[...] = total.astype(BF)

    out = []
    for b, *_ in groups:
        out += [like(b.shape[0] // 2, b.shape[1])] * 2 if split else [like(*b.shape)]
    return call(kernel, out, *blocks, after=after)


def hidden_of_lanes(core, x, zh, y):
    row = jnp.arange(512, dtype=jnp.int32)
    at = functools.partial(turned, core)
    a = (at(zh, row >> 3) * 4 + at(y, row >> 5)) * 64 + at(x, row >> 7) * 4
    b = (at(zh, row >> 3) * 4 + at(y, row >> 7)) * 64 + at(x, row >> 5) * 4 + 16
    both = jnp.stack([a.reshape(4, 128), b.reshape(4, 128)], axis=1).reshape(1024)
    return both + core * 32 + jnp.concatenate([row, row]) % 4


def hidden_work(blocks, picked, cots, scale, after=()):
    rows, width = picked.shape
    count = len(blocks)

    def kernel(*refs):
        picked_ref, scale_ref = refs[:2]
        pre_ref = refs[-1]
        for n in range(count):
            a_ref, b_ref, cot = refs[2 + 3 * n : 5 + 3 * n]
            act, grad = refs[2 + 3 * count + 2 * n :][:2]
            is_gate = lax.broadcasted_iota(jnp.int32, (1, 256), 1) & 4 == 0
            pre_ref[...] = lax.dot_general(
                picked_ref[...],
                jnp.concatenate([a_ref[...], b_ref[...]], axis=0),
                (((1,), (1,)), ((), ())),
                preferred_element_type=F32,
            )
            for r in range(0, rows, 128):
                here = pl.ds(r, 128)
                pre = pre_ref[here, :]
                gate, upval = pre, pltpu.roll(pre, 252, 1)
                weight = scale_ref[here, :]
                sigma = jax.nn.sigmoid(gate)
                act[here, :] = jnp.where(is_gate, weight * gate * sigma * upval, 0.0).astype(BF)
                scaled = cot[here, :].astype(F32) * weight
                up_grad = scaled * gate * sigma
                gate_grad = scaled * upval * sigma * (1.0 + gate * (1.0 - sigma))
                both = jnp.where(is_gate, gate_grad, pltpu.roll(up_grad, 4, 1))
                grad[here, :] = both.astype(BF)

    args = [v for (a, b), cot in zip(blocks, cots) for v in (a, b, cot)]
    out = [like(rows, 256)] * (2 * count)
    flops = 2 * rows * 256 * width * count
    scratch = [pltpu.VMEM((rows, 256), F32)]
    out = call(kernel, out, picked, scale, *args, after=after, flops=flops, scratch=scratch, room=6 * 2**20)
    return out[::2], out[1::2]


def chosen(names_ref, count):
    token = lax.broadcasted_iota(jnp.int32, (count, names_ref.shape[1]), 0)
    return (token == names_ref[...]).astype(F32).astype(BF)


def pick_rows(tokens, names, after=()):
    def kernel(tokens_ref, names_ref, out_ref):
        choice = chosen(names_ref, tokens.shape[0])
        for column in range(0, tokens.shape[1], 512):
            here = pl.ds(column, 512)
            out_ref[:, here] = lax.dot_general(
                choice,
                tokens_ref[:, here],
                (((0,), (0,)), ((), ())),
                preferred_element_type=F32,
            ).astype(BF)

    flops = 2 * tokens.size * names.shape[1]
    (out,) = call(
        kernel, [like(names.shape[1], tokens.shape[1])], tokens, names, after=after, flops=flops, room=2**22
    )
    return out


def slot_part(grads, pieces, count, after=()):
    width = pieces[0].shape[1]

    def kernel(*refs):
        own_ref, other_ref = refs[12:]
        for column in range(0, width, 512):
            here = pl.ds(column, 512)
            part = 0.0
            for n in range(4):
                a_ref, b_ref = refs[4 + 2 * n : 6 + 2 * n]
                part += jnp.dot(
                    refs[n][...],
                    jnp.concatenate([a_ref[:, here], b_ref[:, here]], axis=0),
                    preferred_element_type=F32,
                )
            own_ref[:, here] = part[:count]
            other_ref[:, here] = part[count:].astype(BF)

    out = [like(count, width, F32), like(count, width)]
    return call(kernel, out, *grads, *pieces, after=after, room=6 * 2**20)


def to_tokens(own, arrived, names, tokens, after=()):
    width = own.shape[1]

    def kernel(own_ref, arrived_ref, names_ref, out, tag):
        tag[...] = jnp.zeros(tag.shape, BF)
        choice = chosen(names_ref, tokens)
        for column in range(0, width, 512):
            here = pl.ds(column, 512)
            total = (own_ref[:, here] + arrived_ref[:, here].astype(F32)).astype(BF)
            part = jnp.dot(choice, total, preferred_element_type=F32)
            out[:, here] = part.astype(BF)

    out = [like(tokens, width), like(16, 128)]
    return call(kernel, out, own, arrived, names, after=after, room=6 * 2**20)


def behind(blocks, after):
    count = len(blocks)
    return pl.pallas_call(
        lambda *refs: None,
        out_shape=[like(*b.shape, b.dtype) for b in blocks],
        in_specs=[ANY] * (count + len(after)),
        out_specs=[ANY] * count,
        input_output_aliases={n: n for n in range(count)},
        cost_estimate=pl.CostEstimate(flops=0, bytes_accessed=1, transcendentals=0),
    )(*blocks, *after)


def weight_part(grads, picked, factor, after=()):
    width = picked.shape[1]

    def kernel(picked_ref, *refs):
        for n in range(len(grads)):
            a_ref, b_ref = refs[len(grads) + 2 * n :][:2]
            for column in range(0, width, 512):
                here = pl.ds(column, 512)
                part = lax.dot_general(
                    refs[n][...],
                    picked_ref[:, here],
                    (((0,), (0,)), ((), ())),
                    preferred_element_type=F32,
                )
                a_ref[:, here] = (part[:128] * factor).astype(BF)
                b_ref[:, here] = (part[128:] * factor).astype(BF)

    flops = 2 * picked.size * 256 * len(grads)
    out = [like(128, width)] * (2 * len(grads))
    return call(kernel, out, picked, *grads, after=after, flops=flops, room=6 * 2**20)


def local(tokens, slot_tokens, slot_counts, route_weight, cotangent, weights):
    core, x = lax.axis_index("c"), lax.axis_index("x")
    zh, y = lax.axis_index("zh"), lax.axis_index("y")
    slots = slot_tokens.shape[0]
    width = tokens.shape[1]
    factor = 1.0 / (slots * 256) ** 0.5

    row = jnp.arange(16, dtype=jnp.int32)
    group = jnp.where(row < 8, x, 4 + x)
    wanted = ((row >> 2) & 1) * 64 + core * 32 + group * 4 + row % 4
    choose = (wanted[:, None] == jnp.arange(128, dtype=jnp.int32)[None]).astype(BF)
    own = jnp.dot(choose, weights.reshape(128, width), preferred_element_type=F32).astype(BF)

    names = slot_tokens.reshape(1, slots)
    used = (jnp.arange(slots, dtype=jnp.int32) < slot_counts[0]).astype(F32)
    scale_own = (route_weight * used).reshape(2, 128)

    cot_other = swap(cotangent, "c")
    picked_own = pick_rows(tokens, names, after=[own])
    (own,) = join(own, swap(own, "zh", 0), after=[picked_own])
    a, b = join_parts(own, swap(own, "zh", 1), after=[cot_other])
    picked_other = swap(*behind([picked_own], [a]), "c")
    a, b = join(a, swap(a, "y", 0), b, swap(b, "x", 0))
    scale_other = swap(*behind([scale_own], [a]), "c")
    lanes = lax.optimization_barrier(hidden_of_lanes(core, x, zh, y))
    lanes_other = lax.optimization_barrier(hidden_of_lanes(1 - core, x, zh, y))
    hidden = jnp.arange(1024, dtype=jnp.int32)
    spread = (hidden[:, None] == lanes[None]).astype(BF)
    cot = jnp.dot(
        jnp.concatenate([cotangent, cot_other], axis=0), spread, preferred_element_type=F32
    ).astype(BF)
    cots = [cot[:, 256 * n : 256 * (n + 1)] for n in range(4)]

    a, b = join(a, swap(a, "y", 1), b, swap(b, "x", 1), after=[*cots, scale_other])
    scale = jnp.concatenate([scale_own, scale_other], axis=0).reshape(2 * slots, 1)
    a1, b1, a2, b2 = swap(a, "x", 0), swap(b, "y", 0), swap(a, "x", 1), swap(b, "y", 1)

    picked = jnp.concatenate([picked_own, picked_other], axis=0)
    acts0, grads0 = hidden_work([(a, b)], picked, cots[:1], scale)
    a_own, b_own = weight_part(grads0, picked, factor)
    a1, b1 = behind([a1, b1], [a_own])
    a3, b3 = swap(a1, "x", 1), swap(b1, "y", 1)
    acts1, grads1 = hidden_work([(a1, b1), (a2, b2)], picked, cots[1:3], scale)
    a_mid, b_mid, a_near, b_near = weight_part(grads1, picked, factor)
    acts3, grads3 = hidden_work([(a3, b3)], picked, cots[3:], scale, after=[a_near])
    acts = [*acts0, *acts1, *acts3]
    grads = [*grads0, *grads1, *grads3]
    pieces = [a, b, a1, b1, a2, b2, a3, b3]

    a_far, b_far = weight_part(grads3, picked, factor)
    a_in, b_in = swap(a_far, "x", 1), swap(b_far, "y", 1)
    a_direct, b_direct = swap(a_near, "x", 1), swap(b_near, "y", 1)
    a_mid, b_mid = add(
        [a_mid, a_in], [b_mid, b_in], split=False
    )
    slot_own, slot_other = slot_part(grads, pieces, slots, after=[a_mid])
    grad_other = swap(slot_other, "c")
    act = jnp.concatenate(acts, axis=1)
    act_other = swap(act[slots:], "c")

    gate_lane = (jnp.arange(1024, dtype=jnp.int32) & 4 == 0)[:, None]
    back = ((hidden[None] == lanes[:, None]) & gate_lane).astype(BF)
    back_other = ((hidden[None] == lanes_other[:, None]) & gate_lane).astype(BF)
    activation = (
        jnp.dot(act[:slots], back, preferred_element_type=F32)
        + jnp.dot(act_other, back_other, preferred_element_type=F32)
    ).astype(BF)
    token_grad, tag = to_tokens(slot_own, grad_other, names, tokens.shape[0])

    a_in, b_in = swap(a_mid, "x", 0), swap(b_mid, "y", 0)
    a_own, a_send, b_own, b_send = add([a_own, a_direct, a_in], [b_own, b_direct, b_in])
    a_in, b_in = swap(a_send, "y", 1), swap(b_send, "x", 1)
    a_own, a_send, b_own, b_send = add([a_own, a_in], [b_own, b_in])
    a_in, b_in = swap(a_send, "y", 0), swap(b_send, "x", 0)
    own, send = add_parts(a_own, a_in, b_own, b_in)
    own, send = add([own, swap(send, "zh", 1)], after=[tag])
    (total,) = add([own, swap(send, "zh", 0)], split=False, after=[activation])
    (total,) = add([total, swap(total, "zl")], split=False)
    (total,) = join(total, swap(total, "x", 0))
    (total,) = join(total, swap(total, "x", 1))
    other = swap(total, "c")
    column = jnp.arange(128, dtype=jnp.int32)
    holder = jnp.where(column < 64, core, 1 - core)
    group = ((column >> 3) & 1) * 4 + turned(holder, x, column >> 4)
    place = ((column >> 2) & 1) * 64 + holder * 32 + group * 4 + column % 4
    choose = (jnp.arange(128, dtype=jnp.int32)[:, None] == place[None]).astype(BF)
    weight_grad = jnp.dot(
        choose, jnp.concatenate([total, other], axis=0), preferred_element_type=F32
    ).reshape(2, 64, width)
    return activation, token_grad, weight_grad


def solution(mesh):
    fine = Mesh(mesh.devices.reshape(SIZES), AXES)
    rows = P(AXES, None)
    panel = P(None, ("zh", "y"), None)
    return jax.shard_map(
        local,
        mesh=fine,
        in_specs=(rows, P(AXES), P(AXES), P(AXES), rows, panel),
        out_specs=(rows, rows, panel),
        check_vma=False,
    )
```
